32 devices in a mesh: dp: 8 (over z, x), bin: 4 (over y, core).
Axes of the slice: x: 2, y: 2, z: 4, core: 2. Of those that a mesh axis runs over, the one named last changes fastest.
Arguments:
- features: bfloat16 [4096, 2, 2048], P(('dp', 'bin')), may hold values from -90 to 90
- head_weight: bfloat16 [2048, 1024], P('bin'), may hold values from -9 to 9
- bin_of_row: int32 [4096, 1], P(('dp', 'bin')), may hold values from 0 to 11; in each aligned block of 128 rows (0 to 127, 128 to 255, ...) at most 21 rows name the same one
- bin_owner: int32 [12], replicated, may hold values from 0 to 7, never falling along the last dimension, each value on 1 to 2 neighbouring positions
- bin_link: int32 [12], replicated, may hold values 0 or 1
Outputs:
- grad_rows: bfloat16 [4096, 2, 1024], P(('dp', 'bin'))
- grad_weight: float32 [2048, 1024], P(('bin', 'dp'))
The draws below stay inside these ranges and needn't reach their ends.
Inputs may be any that keep to these rules, and one draw needn't show every extreme that they name: `bin_of_row`: in the rows of one device no bin appears more than 21 times. `bin_owner`: never falls; every owner holds 1 to 2 consecutive bins.
All inputs are finite; a program needn't handle non-finite values.
Results may differ from the reference program's by a relative error of at most 0.012.
Values may be sent and summed in bfloat16 or wider, within the bound.
A program may use at most 64 MiB of HBM per device.

```python
import math
import jax
import jax.numpy as jnp
import numpy as np
from jax import lax

F = 2048
D = 1024
ROWS_DEV = 128
MOSTB = 2
NBINS = 12
CAP = 21
ROWS = 4096
N_DP = 8
N_BIN = 4


def draw_features(key, part):
    parts_of_key = jax.random.split(key, 3)
    base = jnp.clip(jax.random.normal(parts_of_key[0], (ROWS, F)), -5.0, 5.0)
    noise = jnp.clip(jax.random.normal(parts_of_key[1], (ROWS, F)), -5.0, 5.0)
    spread = jnp.exp(jax.random.uniform(parts_of_key[2], (ROWS, 1, 1), minval=0.0, maxval=2.302585))
    other = 0.8 * base + 0.6 * noise
    return (jnp.stack([base, other], axis=1) * spread).astype(jnp.bfloat16)


def draw_head_weight(key, part):
    parts_of_key = jax.random.split(key, 2)
    spread = jnp.exp(jax.random.uniform(parts_of_key[1], (1, D), minval=0.0, maxval=2.302585))
    entries = jnp.clip(jax.random.normal(parts_of_key[0], (F, D)), -5.0, 5.0)
    return (entries * spread / F ** 0.5).astype(jnp.bfloat16)


def with_ends(result, stream_key, smallest, top_value):
    longest = result.shape.index(max(result.shape))
    spots = []
    for shift in (0, 1):
        where = [jax.random.randint(jax.random.fold_in(stream_key, axis), (), 0, length) for axis, length in enumerate(result.shape)]
        where[longest] = (where[longest] + shift) % result.shape[longest]
        spots.append(tuple(where))
    return result.at[spots[0]].set(smallest).at[spots[1]].set(top_value)


def profile(count, total, bound, lean):
    portions = [(1 << 20) // math.isqrt(rank ** lean) + 1 for rank in range(2, count + 1)]
    spare, counts = total - bound - (count - 1), [1] * (count - 1)
    while spare > 0:
        candidates = [i for i in range(count - 1) if counts[i] < bound]
        whole, remaining = sum([portions[i] for i in candidates]), spare
        for i in candidates:
            more = min(bound - counts[i], max(1, remaining * portions[i] // whole), spare)
            counts[i] = counts[i] + more
            spare = spare - more
    return np.array([bound] + counts)


def uneven(stream_key, amount, total, most, lean):
    if amount == 2:
        one = jax.random.randint(stream_key, (), max(1, total - most), min(most, total - 1) + 1)
        return jnp.stack([one, total - one])
    sizes = jnp.asarray(profile(amount, total, most, lean), jnp.int32)
    pairs = (amount - 1) // 2
    source_of, taker = sizes[1:1 + 2 * pairs:2], sizes[2:2 + 2 * pairs:2]
    room = jnp.minimum(source_of - 1, most - taker)
    moved = jax.random.randint(jax.random.fold_in(stream_key, 1), (pairs,), 0, 1 << 20) % (room + 1)
    sizes = sizes.at[1:1 + 2 * pairs:2].set(source_of - moved).at[2:2 + 2 * pairs:2].set(taker + moved)
    return sizes[jax.random.permutation(jax.random.fold_in(stream_key, 2), amount)]


def deal_out(stream_key, own, number, rows, amount, top, limit, lean):
    ranking = jax.random.permutation(stream_key, amount)
    heavy_load, usual = load_shares(amount, rows * top, limit, lean, True), load_shares(amount, rows * top, limit, lean, False)
    places = jnp.arange(amount)

    def named(lengths, rotation):
        used = int((lengths > 0).sum())
        fixed = max(1, used // 4)
        shifted = fixed + (places - fixed + rotation * (used - fixed)) % max(1, amount - fixed)
        return jnp.zeros((amount,), jnp.int32).at[ranking[jnp.where(places < fixed, places, shifted)]].set(jnp.asarray(lengths, jnp.int32))

    lengths = jnp.where(number % 4 == 0, named(heavy_load, number // 4), named(usual, number - number // 4 - 1))
    mixed = jax.random.permutation(jax.random.fold_in(own, 3), amount)
    donor, sink = mixed[0:amount // 2 * 2:2], mixed[1:amount // 2 * 2:2]
    slack = jnp.minimum(lengths[donor] - 1, limit - lengths[sink]) // 2
    slack = jnp.where((donor == ranking[0]) | (sink == ranking[0]) | (lengths[sink] == 0), 0, jnp.maximum(slack, 0))
    shifted = jax.random.randint(jax.random.fold_in(own, 4), (amount // 2,), 0, 1 << 20) % (slack + 1)
    lengths = lengths.at[donor].add(-shifted).at[sink].add(shifted)
    items = jnp.searchsorted(jnp.cumsum(lengths), jnp.arange(rows * top), side="right").astype(jnp.int32)
    table = items.reshape(top, rows).T
    table = table[jax.random.permutation(jax.random.fold_in(own, 1), rows)]
    rotation = jax.random.randint(jax.random.fold_in(own, 2), (rows, 1), 0, top)
    return jnp.take_along_axis(table, (jnp.arange(top)[None, :] + rotation) % top, axis=1)


def load_shares(number_of, total, reach, slope, full):
    portions = [(1 << 20) // math.isqrt(standing ** slope) + 1 for standing in range(1, number_of + 1)]
    largest = reach if full else min(reach, max(-(-total // number_of), total * portions[0] // sum(portions)))
    least = 1 if total - largest >= number_of - 1 else 0
    given, surplus = [largest] + [least] * (number_of - 1), total - largest - least * (number_of - 1)
    while surplus > 0:
        movable = [i for i in range(1, number_of) if given[i] < largest] or [i for i in range(1, number_of) if given[i] < reach]
        pool, budget = sum([portions[i] for i in movable]), surplus
        for i in movable:
            more = min(reach - given[i], max(1, budget * portions[i] // pool), surplus)
            given[i] = given[i] + more
            surplus = surplus - more
    return np.array(given)


def setup_inputs(seed: int = 0) -> dict:
    keys = jax.random.split(jax.random.key(seed), 6)
    features = draw_features(jax.random.fold_in(keys[5], 71), 0)
    head_weight = draw_head_weight(jax.random.fold_in(keys[5], 71), 0)
    bin_of_row_keys = jax.random.split(jax.random.fold_in(keys[2], 1), ROWS // ROWS_DEV)
    bin_of_row_turns = jax.random.permutation(jax.random.fold_in(keys[2], 3), ROWS // ROWS_DEV)
    bin_of_row = jax.vmap(lambda own, number: deal_out(jax.random.fold_in(keys[2], 2), own, number, ROWS_DEV, NBINS, 1, CAP, 2))(bin_of_row_keys, bin_of_row_turns).reshape((ROWS, 1))
    bin_owner = jnp.searchsorted(jnp.cumsum(uneven(keys[3], N_DP, NBINS, MOSTB, 1)), jnp.arange(NBINS), side="right").astype(jnp.int32)
    bin_link = with_ends((jax.random.randint(keys[4], (NBINS,), 0, 2) < 1).astype(jnp.int32), jax.random.fold_in(keys[4], 1), 0, 1)
    return {"features": features, "head_weight": head_weight, "bin_of_row": bin_of_row, "bin_owner": bin_owner, "bin_link": bin_link}


SOFTMAX_TEMP_SCALE = 0.1

def allowed_mask(valid, first, bin_link, group_slots, per_bin):
    per_owner = per_bin * MOSTB
    position = jnp.arange(group_slots, dtype=jnp.int32)
    local_bin = position % per_owner // per_bin
    padded = jnp.concatenate([bin_link.astype(jnp.int32), jnp.zeros((MOSTB,), jnp.int32)])
    nearby = lax.dynamic_slice(padded, (first,), (MOSTB,))
    lower = jnp.minimum(local_bin[:, None], local_bin[None, :])
    linked = jnp.zeros((group_slots, group_slots), jnp.int32)
    for height in range(MOSTB):
        linked = linked + jnp.where(lower == height, nearby[height], 0)
    spacing = jnp.abs(local_bin[:, None] - local_bin[None, :])
    paired = valid[:, None] & valid[None, :]
    allowed = paired & ((spacing == 0) | (spacing == 1) & (linked == 1))
    allowed = allowed | (position[:, None] == position[None, :])
    return allowed.astype(jnp.float32)

def contrast(query_rows, key_matrix, allowed, valid):
    similarity_scores = lax.dot_general(query_rows, key_matrix, (((1,), (1,)), ((), ())), preferred_element_type=jnp.float32) / SOFTMAX_TEMP_SCALE
    weights = allowed * jnp.exp(similarity_scores)
    shares = weights / lax.optimization_barrier(jnp.sum(weights, axis=1, keepdims=True))
    position = jnp.arange(query_rows.shape[0], dtype=jnp.int32)
    diagonal = (position[:, None] == position[None, :]).astype(jnp.float32)
    logit_gradient = ((shares - diagonal) * valid[:, None]).astype(jnp.bfloat16)
    query_gradient = (jnp.dot(logit_gradient, key_matrix, preferred_element_type=jnp.float32) / SOFTMAX_TEMP_SCALE).astype(jnp.bfloat16)
    key_gradient_rows = (lax.dot_general(logit_gradient, query_rows, (((0,), (0,)), ((), ())), preferred_element_type=jnp.float32) / SOFTMAX_TEMP_SCALE).astype(jnp.bfloat16)
    return jnp.stack([query_gradient, key_gradient_rows], axis=1)

def reference(features, head_weight, bin_of_row, bin_owner, bin_link):
    per_owner = CAP * MOSTB
    group_slots = N_DP * per_owner
    embedded = jnp.dot(features.reshape(ROWS * 2, F), head_weight, preferred_element_type=jnp.float32).reshape(ROWS, 2, D)
    scale = lax.rsqrt(lax.optimization_barrier(jnp.sum(embedded * embedded, axis=2, keepdims=True)) + 1e-06)
    unit = embedded * scale
    sent = unit.astype(jnp.bfloat16)
    row_bins = bin_of_row[:, 0].astype(jnp.int32)
    owner = bin_owner[row_bins].astype(jnp.int32)
    first_by_bin = lax.optimization_barrier(jnp.sum((bin_owner[None, :] < bin_owner[:, None]).astype(jnp.int32), axis=1)).astype(jnp.int32)
    local_bin = row_bins - first_by_bin[row_bins]
    per_device = row_bins.reshape(N_DP * N_BIN, ROWS_DEV)
    order = jnp.arange(ROWS_DEV, dtype=jnp.int32)
    earlier = (per_device[:, :, None] == per_device[:, None, :]) & (order[None, None, :] < order[None, :, None])
    seat = lax.optimization_barrier(jnp.sum(earlier.astype(jnp.int32), axis=2)).reshape(ROWS).astype(jnp.int32)
    device = jnp.arange(ROWS, dtype=jnp.int32) // ROWS_DEV
    group = owner * N_BIN + device % N_BIN
    position = (group * group_slots + device // N_BIN * per_owner + local_bin * CAP + seat).astype(jnp.int32)
    row_of = jnp.full((N_DP * N_BIN * group_slots,), ROWS, jnp.int32).at[position].set(jnp.arange(ROWS, dtype=jnp.int32))
    padded = jnp.concatenate([sent, jnp.zeros((1, 2, D), jnp.bfloat16)], axis=0)

    def visit(carry, index):
        members = lax.dynamic_slice(row_of, (index * group_slots,), (group_slots,))
        valid = members < ROWS
        first = jnp.sum((bin_owner < index // N_BIN).astype(jnp.int32)).astype(jnp.int32)
        allowed = allowed_mask(valid, first, bin_link, group_slots, CAP)
        picked = padded[members]
        grads = contrast(picked[:, 0], picked[:, 1], allowed, valid.astype(jnp.float32))
        return (carry.at[members].set(grads), None)
    start = jnp.zeros((ROWS + 1, 2, D), jnp.bfloat16)
    grads_pad, _ = lax.scan(visit, start, jnp.arange(N_DP * N_BIN, dtype=jnp.int32))
    row_grads = grads_pad[:ROWS].astype(jnp.float32)
    grad_rows = (scale * (row_grads - unit * lax.optimization_barrier(jnp.sum(unit * row_grads, axis=2, keepdims=True)))).astype(jnp.bfloat16)
    grad_weight = lax.dot_general(features.reshape(ROWS * 2, F), grad_rows.reshape(ROWS * 2, D), (((0,), (0,)), ((), ())), preferred_element_type=jnp.float32) / ROWS_DEV
    return (grad_rows, grad_weight)
```

```python
import functools

import jax
import jax.numpy as jnp
from jax import lax
from jax.experimental import pallas as pl
from jax.experimental.pallas import tpu as pltpu
from jax.sharding import PartitionSpec as P

MOSTB = 2


SOFTMAX_TEMP_SCALE = 0.1


def allowed_mask(valid, first, bin_link, group_slots, per_bin):
    per_owner = per_bin * MOSTB
    position = jnp.arange(group_slots, dtype=jnp.int32)
    local_bin = position % per_owner // per_bin
    padded = jnp.concatenate([bin_link, jnp.zeros((MOSTB,), jnp.int32)])
    nearby = lax.dynamic_slice(padded, (first,), (MOSTB,))
    lower = jnp.minimum(local_bin[:, None], local_bin[None, :])
    linked = jnp.zeros((group_slots, group_slots), jnp.int32)
    for height in range(MOSTB):
        linked = linked + jnp.where(lower == height, nearby[height], 0)
    spacing = jnp.abs(local_bin[:, None] - local_bin[None, :])
    paired = valid[:, None] & valid[None, :]
    allowed = paired & ((spacing == 0) | (spacing == 1) & (linked == 1))
    allowed = allowed | (position[:, None] == position[None, :])
    return allowed.astype(jnp.float32)


def contrast(query_rows, key_matrix, allowed, valid):
    similarity_scores = (
        lax.dot_general(
            query_rows, key_matrix, (((1,), (1,)), ((), ())), preferred_element_type=jnp.float32
        )
        / SOFTMAX_TEMP_SCALE
    )
    weights = allowed * jnp.exp(similarity_scores)
    shares = weights / jnp.sum(weights, axis=1, keepdims=True)
    position = jnp.arange(query_rows.shape[0], dtype=jnp.int32)
    diagonal = (position[:, None] == position[None, :]).astype(jnp.float32)
    logit_gradient = ((shares - diagonal) * valid[:, None]).astype(jnp.bfloat16)
    query_gradient = (
        jnp.dot(logit_gradient, key_matrix, preferred_element_type=jnp.float32) / SOFTMAX_TEMP_SCALE
    ).astype(jnp.bfloat16)
    key_gradient_rows = (
        lax.dot_general(
            logit_gradient, query_rows, (((0,), (0,)), ((), ())), preferred_element_type=jnp.float32
        )
        / SOFTMAX_TEMP_SCALE
    ).astype(jnp.bfloat16)
    return jnp.stack([query_gradient, key_gradient_rows], axis=1)


def local(features, head_weight, bin_of_row, bin_owner, bin_link):
    rows_dev, views, feat_dim = features.shape
    part_rows, emb_dim = head_weight.shape
    sources = lax.axis_size("dp")
    bin_count = bin_owner.shape[0]
    per_bin = max(2, 2 * rows_dev // bin_count)
    per_owner = per_bin * MOSTB
    group_slots = sources * per_owner
    flat = features.reshape(rows_dev * views, feat_dim)
    columns = flat
    folded = jnp.dot(
        columns,
        lax.all_gather(head_weight, "bin", axis=0, tiled=True),
        preferred_element_type=jnp.float32,
    )
    embedded = folded.reshape(rows_dev, views, emb_dim)
    scale = lax.rsqrt(jnp.sum(embedded * embedded, axis=2, keepdims=True) + 1e-06)
    unit = embedded * scale
    sent = unit.astype(jnp.bfloat16)
    row_bins = bin_of_row[:, 0]
    lookup = row_bins[:, None] == jnp.arange(bin_count, dtype=jnp.int32)[None, :]
    owner = jnp.sum(jnp.where(lookup, bin_owner[None, :], 0), axis=1)
    first_by_bin = jnp.sum((bin_owner[None, :] < bin_owner[:, None]).astype(jnp.int32), axis=1)
    local_bin = row_bins - jnp.sum(jnp.where(lookup, first_by_bin[None, :], 0), axis=1)
    order = jnp.arange(rows_dev, dtype=jnp.int32)
    earlier = (row_bins[:, None] == row_bins[None, :]) & (order[None, :] < order[:, None])
    seat = jnp.sum(earlier.astype(jnp.int32), axis=1)
    target = owner * per_owner + local_bin * per_bin + seat
    outbox = jnp.zeros((group_slots, views, emb_dim), jnp.bfloat16).at[target].set(sent)
    filled = (
        jnp.zeros((group_slots,), jnp.bfloat16).at[target].set(jnp.ones((rows_dev,), jnp.bfloat16))
    )
    inbox, present = (
        lax.all_to_all(
            outbox.reshape(sources, per_owner, views, emb_dim),
            "dp",
            split_axis=0,
            concat_axis=0,
            tiled=True,
        ),
        lax.all_to_all(
            filled.reshape(sources, per_owner), "dp", split_axis=0, concat_axis=0, tiled=True
        ),
    )
    inbox = inbox.reshape(group_slots, views, emb_dim)
    valid = present.reshape(group_slots) > 0.5
    first = jnp.sum((bin_owner < lax.axis_index("dp")).astype(jnp.int32))
    allowed = allowed_mask(valid, first, bin_link, group_slots, per_bin)
    grads = contrast(inbox[:, 0], inbox[:, 1], allowed, valid.astype(jnp.float32))
    returned = lax.all_to_all(
        grads.reshape(sources, per_owner, views, emb_dim),
        "dp",
        split_axis=0,
        concat_axis=0,
        tiled=True,
    )
    row_grads = returned.reshape(group_slots, views, emb_dim)[target].astype(jnp.float32)
    grad_rows = (
        scale * (row_grads - unit * jnp.sum(unit * row_grads, axis=2, keepdims=True))
    ).astype(jnp.bfloat16)
    column_start = lax.axis_index("bin") * part_rows
    trunk = lax.all_gather(features, "bin", axis=0, tiled=True)
    outgrad = lax.all_gather(grad_rows, "bin", axis=0, tiled=True)
    columns = lax.dynamic_slice_in_dim(trunk, column_start, part_rows, 2)
    count = trunk.shape[0]
    local_grad = lax.dot_general(
        columns.reshape(count * views, part_rows),
        outgrad.reshape(count * views, emb_dim),
        (((0,), (0,)), ((), ())),
        preferred_element_type=jnp.float32,
    )
    grad_weight = lax.psum_scatter(local_grad, "dp", scatter_dimension=0, tiled=True) / rows_dev
    return (grad_rows, grad_weight)


CHUNKS = 4
MESH = pl.DeviceIdType.MESH
F32 = jnp.float32
BF16 = jnp.bfloat16


def owners_kernel(
    n_dp, block, per_bin, rows_dev,
    feat, weight, row_bin, bin_owner, bin_link,
    out_rows, out_weight,
    wbuf, fcols, outbox, inbox, flag_out, flag_in, grads, returned, gathered, terms, landed,
    w_send, w_recv, f_send, f_recv, flag_send, flag_recv, a_send, a_recv,
    b_send, b_recv, g_send, g_recv, r_send, r_recv,
):
    dp = lax.axis_index("dp")
    col = lax.axis_index("bin")
    half, core = col // 2, col % 2
    sib = half * 2 + (1 - core)
    peer = (1 - half) * 2 + core
    diag = (1 - half) * 2 + (1 - core)
    near = (col, sib, peer, diag)
    ahead = [lax.rem(dp + m, n_dp) for m in range(n_dp)]
    behind = [lax.rem(dp + n_dp - m, n_dp) for m in range(n_dp)]
    rows2, feat_dim = feat.shape
    part = weight.shape[0]
    emb = weight.shape[1]
    width = emb // CHUNKS
    slots = n_dp * block
    piece = part // n_dp
    bins = bin_owner.shape[0]
    sends = []

    def push(src, dst, send, recv, device):
        copy = pltpu.make_async_remote_copy(
            src_ref=src, dst_ref=dst, send_sem=send, recv_sem=recv,
            device_id=device, device_id_type=MESH,
        )
        copy.start()
        sends.append(copy)
        return copy

    barrier = pltpu.get_barrier_semaphore()
    for other in near[1:]:
        pl.semaphore_signal(barrier, inc=1, device_id=(dp, other), device_id_type=MESH)
    for m in range(1, n_dp):
        pl.semaphore_signal(barrier, inc=1, device_id=(ahead[m], col), device_id_type=MESH)
    pl.semaphore_wait(barrier, 3 + n_dp - 1)

    lanes = [pl.ds(k * width, width) for k in range(CHUNKS)]
    own_w = []
    for k in range(CHUNKS):
        to_peer = push(
            weight.at[:, lanes[k]], wbuf.at[1, :, lanes[k]],
            w_send.at[1, k], w_recv.at[1, k], (dp, peer),
        )
        to_sib = push(
            weight.at[:, lanes[k]], wbuf.at[0, :, lanes[k]],
            w_send.at[0, k], w_recv.at[0, k], (dp, sib),
        )
        own_w.append((to_sib, to_peer))

    pos = lax.broadcasted_iota(jnp.int32, (rows_dev, rows2), 0)
    lane_row = lax.broadcasted_iota(jnp.int32, (rows_dev, rows2), 1) // 2
    bin_col = jnp.broadcast_to(row_bin[...], (rows_dev, rows2))
    bin_row = jnp.sum(jnp.where(pos == lane_row, bin_col, 0), axis=0, keepdims=True)
    seat = jnp.sum(
        jnp.where((bin_col == bin_row) & (pos < lane_row), 1, 0), axis=0, keepdims=True
    )
    target = seat
    link = jnp.int32(0)
    for b in range(bins):
        owner = bin_owner[b]
        local_bin = jnp.int32(0)
        for b2 in range(b):
            local_bin = local_bin + jnp.where(bin_owner[b2] == owner, 1, 0)
        away = owner - dp
        away = jnp.where(away < 0, away + n_dp, away)
        target = target + jnp.where(bin_row == b, away * block + local_bin * per_bin, 0)
        if b + 1 < bins:
            link = link + jnp.where((owner == dp) & (local_bin == 0), bin_link[b], 0)
    place = lax.broadcasted_iota(jnp.int32, (slots, rows2), 0)
    view = lax.broadcasted_iota(jnp.int32, (slots, rows2), 1) % 2
    here = place == jnp.broadcast_to(target, (slots, rows2))
    pick = [
        jnp.where(here & (view == v), 1.0, 0.0).astype(F32) for v in range(2)
    ]
    flags = jnp.broadcast_to(jnp.sum(pick[0], axis=1, keepdims=True), (slots, 128)).astype(BF16)
    pick = [p.astype(BF16) for p in pick]
    flag_out[...] = flags
    flag_in[0:block, :] = flags[0:block]
    flag_copies = []
    for m in range(1, n_dp):
        span = pl.ds(m * block, block)
        flag_copies.append(push(
            flag_out.at[span], flag_in.at[span], flag_send.at[m], flag_recv.at[m],
            (ahead[m], col),
        ))

    order = list(range(n_dp - 1, 0, -1))

    def start_out(k):
        copies = []
        for m in order:
            span = pl.ds(m * block, block)
            copies.append(push(
                outbox.at[k, :, span, :], inbox.at[k, :, span, :],
                a_send.at[k, m], a_recv.at[k, m], (ahead[m], col),
            ))
        return copies

    def columns_of(other):
        return pl.ds(pl.multiple_of(other * part, part), part)

    out_copies = []
    for k in range(CHUNKS):
        to_sib, to_peer = own_w[k]
        to_peer.wait_recv()
        relay = push(
            wbuf.at[1, :, lanes[k]], wbuf.at[2, :, lanes[k]],
            w_send.at[2, k], w_recv.at[2, k], (dp, sib),
        )
        y = jnp.dot(feat[:, columns_of(col)], weight[:, lanes[k]], preferred_element_type=F32)
        y += jnp.dot(feat[:, columns_of(peer)], wbuf[1, :, lanes[k]], preferred_element_type=F32)
        to_sib.wait_recv()
        y += jnp.dot(feat[:, columns_of(sib)], wbuf[0, :, lanes[k]], preferred_element_type=F32)
        relay.wait_recv()
        y += jnp.dot(feat[:, columns_of(diag)], wbuf[2, :, lanes[k]], preferred_element_type=F32)
        y = y.astype(BF16)
        for v in range(2):
            placed = jnp.dot(pick[v], y, preferred_element_type=F32).astype(BF16)
            outbox[k, v] = placed
            inbox[k, v, 0:block, :] = placed[0:block]
        out_copies.append(start_out(k))

    f_copies = []
    for x in (2, 3, 1):
        f_copies.append(push(
            feat.at[:, columns_of(near[x])], fcols.at[pl.ds(x * rows2, rows2), :],
            f_send.at[x], f_recv.at[x], (dp, near[x]),
        ))
    fcols[0:rows2, :] = feat[:, columns_of(col)]

    for copy in flag_copies:
        copy.wait_recv()
    raw = jnp.zeros((slots, slots), F32)
    square = [jnp.zeros((slots, 1), F32) for _ in range(2)]
    for k in range(CHUNKS):
        for copy in out_copies[k]:
            copy.wait_recv()
        raw += lax.dot_general(
            inbox[k, 0], inbox[k, 1], (((1,), (1,)), ((), ())), preferred_element_type=F32
        )
        for v in range(2):
            row = inbox[k, v].astype(F32)
            square[v] += jnp.sum(row * row, axis=1, keepdims=True)
    scale0 = lax.rsqrt(square[0] + 1e-06)
    scale1 = lax.rsqrt(square[1] + 1e-06)
    s_pos = lax.broadcasted_iota(jnp.int32, (slots, slots), 0)
    t_pos = lax.broadcasted_iota(jnp.int32, (slots, slots), 1)
    eye = s_pos == t_pos
    scale1_row = jnp.sum(jnp.where(eye, scale1, 0.0), axis=0, keepdims=True)
    valid = flag_in[:, 0:1].astype(F32)
    valid_row = jnp.sum(jnp.where(eye, valid, 0.0), axis=0, keepdims=True)
    s_bin = (lax.broadcasted_iota(jnp.int32, (slots, 1), 0) % block >= per_bin).astype(jnp.int32)
    t_bin = (lax.broadcasted_iota(jnp.int32, (1, slots), 1) % block >= per_bin).astype(jnp.int32)
    bound = jnp.where(s_bin == t_bin, 1.0, (link == 1).astype(F32))
    allowed = jnp.where(eye, 1.0, valid * valid_row * bound)
    scores = raw * scale0 * scale1_row / SOFTMAX_TEMP_SCALE
    weights = allowed * jnp.exp(scores)
    shares = weights / jnp.sum(weights, axis=1, keepdims=True)
    logit = (shares - jnp.where(eye, 1.0, 0.0)) * valid
    slope = logit * scores
    lean0 = jnp.sum(slope, axis=1, keepdims=True) * scale0 * scale0
    lean1_row = jnp.sum(slope, axis=0, keepdims=True) * scale1_row * scale1_row
    lean1 = jnp.sum(jnp.where(eye, lean1_row, 0.0), axis=1, keepdims=True)
    mix = (logit * scale0 * scale1_row / SOFTMAX_TEMP_SCALE).astype(BF16)
    mix_t = mix.T

    back_copies = []
    for k in range(CHUNKS):
        y0, y1 = inbox[k, 0], inbox[k, 1]
        g0 = jnp.dot(mix, y1, preferred_element_type=F32) - lean0 * y0.astype(F32)
        g1 = jnp.dot(mix_t, y0, preferred_element_type=F32) - lean1 * y1.astype(F32)
        for v, g in ((0, g0.astype(BF16)), (1, g1.astype(BF16))):
            grads[k, v] = g
            returned[k, v, 0:block, :] = g[0:block]
        copies = []
        for m in order:
            span = pl.ds(m * block, block)
            copies.append(push(
                grads.at[k, :, span, :], returned.at[k, :, span, :],
                b_send.at[k, m], b_recv.at[k, m], (behind[m], col),
            ))
        back_copies.append(copies)

    for copy in f_copies:
        copy.wait_recv()
    sum_copies = []
    for k in range(CHUNKS):
        for copy in back_copies[k]:
            copy.wait_recv()
        rows = jnp.zeros((rows2, width), F32)
        for v in range(2):
            rows += lax.dot_general(
                pick[v], returned[k, v], (((0,), (0,)), ((), ())), preferred_element_type=F32
            )
        rows = rows.astype(BF16)
        out_rows[:, lanes[k]] = rows
        gathered[k, 0:rows2, :] = rows
        own = gathered.at[k, pl.ds(0, rows2), :]
        spans = [pl.ds(x * rows2, rows2) for x in range(4)]
        to_peer = push(
            own, gathered.at[k, spans[2], :], g_send.at[1, k], g_recv.at[1, k], (dp, peer)
        )
        to_sib = push(
            own, gathered.at[k, spans[1], :], g_send.at[0, k], g_recv.at[0, k], (dp, sib)
        )
        to_peer.wait_recv()
        relay = push(
            gathered.at[k, spans[2], :], gathered.at[k, spans[3], :],
            g_send.at[2, k], g_recv.at[2, k], (dp, sib),
        )
        to_sib.wait_recv()
        relay.wait_recv()
        term = lax.dot_general(
            fcols[...], gathered[k], (((0,), (0,)), ((), ())), preferred_element_type=F32
        )
        terms[k] = term.astype(BF16)
        copies = []
        for m in order:
            span = pl.ds(pl.multiple_of(ahead[m] * piece, piece), piece)
            copies.append(push(
                terms.at[k, span, :], landed.at[k, m], r_send.at[k, m], r_recv.at[k, m],
                (ahead[m], col),
            ))
        sum_copies.append(copies)
    mine = pl.ds(pl.multiple_of(dp * piece, piece), piece)
    for k in range(CHUNKS):
        total = terms[k, mine, :].astype(F32)
        for copy in sum_copies[k]:
            copy.wait_recv()
        for m in range(1, n_dp):
            total += landed[k, m].astype(F32)
        out_weight[:, lanes[k]] = total / rows_dev
    for copy in sends:
        copy.wait_send()


def local_kernel(features, head_weight, bin_of_row, bin_owner, bin_link):
    rows_dev, views, feat_dim = features.shape
    part, emb = head_weight.shape
    n_dp = lax.axis_size("dp")
    bins = bin_owner.shape[0]
    per_bin = max(2, 2 * rows_dev // bins)
    block = -(-per_bin * MOSTB // 16) * 16
    slots = n_dp * block
    rows2 = rows_dev * views
    width = emb // CHUNKS
    piece = part // n_dp
    vmem = pl.BlockSpec(memory_space=pltpu.VMEM)
    smem = pl.BlockSpec(memory_space=pltpu.SMEM)
    dma = pltpu.SemaphoreType.DMA
    wide = pltpu.VMEM((CHUNKS, views, slots, width), BF16)
    grad_rows, grad_weight = pl.pallas_call(
        functools.partial(owners_kernel, n_dp, block, per_bin, rows_dev),
        out_shape=(
            jax.ShapeDtypeStruct((rows2, emb), BF16),
            jax.ShapeDtypeStruct((piece, emb), F32),
        ),
        in_specs=[vmem, vmem, vmem, smem, smem],
        out_specs=(vmem, vmem),
        scratch_shapes=[
            pltpu.VMEM((3, part, emb), BF16),
            pltpu.VMEM((4 * rows2, part), BF16),
            wide, wide,
            pltpu.VMEM((slots, 128), BF16),
            pltpu.VMEM((slots, 128), BF16),
            wide, wide,
            pltpu.VMEM((CHUNKS, 4 * rows2, width), BF16),
            pltpu.VMEM((CHUNKS, part, width), BF16),
            pltpu.VMEM((CHUNKS, n_dp, piece, width), BF16),
            dma((3, CHUNKS)), dma((3, CHUNKS)),
            dma((4,)), dma((4,)),
            dma((n_dp,)), dma((n_dp,)),
            dma((CHUNKS, n_dp)), dma((CHUNKS, n_dp)),
            dma((CHUNKS, n_dp)), dma((CHUNKS, n_dp)),
            dma((3, CHUNKS)), dma((3, CHUNKS)),
            dma((CHUNKS, n_dp)), dma((CHUNKS, n_dp)),
        ],
        compiler_params=pltpu.CompilerParams(
            collective_id=0, has_side_effects=True, vmem_limit_bytes=48 * 1024 * 1024
        ),
        cost_estimate=pl.CostEstimate(
            flops=4 * rows2 * feat_dim * emb, bytes_accessed=16 * 1024 * 1024, transcendentals=0
        ),
    )(features.reshape(rows2, feat_dim), head_weight, bin_of_row, bin_owner, bin_link)
    return grad_rows.reshape(rows_dev, views, emb), grad_weight


def solution(mesh):
    small = mesh.shape["dp"] <= 8 and mesh.shape["bin"] == 4
    return jax.shard_map(
        local_kernel if small else local,
        mesh=mesh,
        in_specs=(P(("dp", "bin"), None, None), P("bin", None), P(("dp", "bin"), None), P(), P()),
        out_specs=(P(("dp", "bin"), None, None), P(("bin", "dp"), None)),
        check_vma=False,
    )
```

```python
import functools

import jax
import jax.numpy as jnp
from jax import lax
from jax.experimental import pallas as pl
from jax.experimental.pallas import tpu as pltpu
from jax.sharding import PartitionSpec as P

MOSTB = 2


SOFTMAX_TEMP_SCALE = 0.1


def allowed_mask(valid, first, bin_link, group_slots, per_bin):
    per_owner = per_bin * MOSTB
    position = jnp.arange(group_slots, dtype=jnp.int32)
    local_bin = position % per_owner // per_bin
    padded = jnp.concatenate([bin_link, jnp.zeros((MOSTB,), jnp.int32)])
    nearby = lax.dynamic_slice(padded, (first,), (MOSTB,))
    lower = jnp.minimum(local_bin[:, None], local_bin[None, :])
    linked = jnp.zeros((group_slots, group_slots), jnp.int32)
    for height in range(MOSTB):
        linked = linked + jnp.where(lower == height, nearby[height], 0)
    spacing = jnp.abs(local_bin[:, None] - local_bin[None, :])
    paired = valid[:, None] & valid[None, :]
    allowed = paired & ((spacing == 0) | (spacing == 1) & (linked == 1))
    allowed = allowed | (position[:, None] == position[None, :])
    return allowed.astype(jnp.float32)


def contrast(query_rows, key_matrix, allowed, valid):
    similarity_scores = (
        lax.dot_general(
            query_rows, key_matrix, (((1,), (1,)), ((), ())), preferred_element_type=jnp.float32
        )
        / SOFTMAX_TEMP_SCALE
    )
    weights = allowed * jnp.exp(similarity_scores)
    shares = weights / jnp.sum(weights, axis=1, keepdims=True)
    position = jnp.arange(query_rows.shape[0], dtype=jnp.int32)
    diagonal = (position[:, None] == position[None, :]).astype(jnp.float32)
    logit_gradient = ((shares - diagonal) * valid[:, None]).astype(jnp.bfloat16)
    query_gradient = (
        jnp.dot(logit_gradient, key_matrix, preferred_element_type=jnp.float32) / SOFTMAX_TEMP_SCALE
    ).astype(jnp.bfloat16)
    key_gradient_rows = (
        lax.dot_general(
            logit_gradient, query_rows, (((0,), (0,)), ((), ())), preferred_element_type=jnp.float32
        )
        / SOFTMAX_TEMP_SCALE
    ).astype(jnp.bfloat16)
    return jnp.stack([query_gradient, key_gradient_rows], axis=1)


def local(features, head_weight, bin_of_row, bin_owner, bin_link):
    rows_dev, views, feat_dim = features.shape
    part_rows, emb_dim = head_weight.shape
    sources = lax.axis_size("dp")
    bin_count = bin_owner.shape[0]
    per_bin = max(2, 2 * rows_dev // bin_count)
    per_owner = per_bin * MOSTB
    group_slots = sources * per_owner
    flat = features.reshape(rows_dev * views, feat_dim)
    columns = flat
    folded = jnp.dot(
        columns,
        lax.all_gather(head_weight, "bin", axis=0, tiled=True),
        preferred_element_type=jnp.float32,
    )
    embedded = folded.reshape(rows_dev, views, emb_dim)
    scale = lax.rsqrt(jnp.sum(embedded * embedded, axis=2, keepdims=True) + 1e-06)
    unit = embedded * scale
    sent = unit.astype(jnp.bfloat16)
    row_bins = bin_of_row[:, 0]
    lookup = row_bins[:, None] == jnp.arange(bin_count, dtype=jnp.int32)[None, :]
    owner = jnp.sum(jnp.where(lookup, bin_owner[None, :], 0), axis=1)
    first_by_bin = jnp.sum((bin_owner[None, :] < bin_owner[:, None]).astype(jnp.int32), axis=1)
    local_bin = row_bins - jnp.sum(jnp.where(lookup, first_by_bin[None, :], 0), axis=1)
    order = jnp.arange(rows_dev, dtype=jnp.int32)
    earlier = (row_bins[:, None] == row_bins[None, :]) & (order[None, :] < order[:, None])
    seat = jnp.sum(earlier.astype(jnp.int32), axis=1)
    target = owner * per_owner + local_bin * per_bin + seat
    outbox = jnp.zeros((group_slots, views, emb_dim), jnp.bfloat16).at[target].set(sent)
    filled = (
        jnp.zeros((group_slots,), jnp.bfloat16).at[target].set(jnp.ones((rows_dev,), jnp.bfloat16))
    )
    inbox, present = (
        lax.all_to_all(
            outbox.reshape(sources, per_owner, views, emb_dim),
            "dp",
            split_axis=0,
            concat_axis=0,
            tiled=True,
        ),
        lax.all_to_all(
            filled.reshape(sources, per_owner), "dp", split_axis=0, concat_axis=0, tiled=True
        ),
    )
    inbox = inbox.reshape(group_slots, views, emb_dim)
    valid = present.reshape(group_slots) > 0.5
    first = jnp.sum((bin_owner < lax.axis_index("dp")).astype(jnp.int32))
    allowed = allowed_mask(valid, first, bin_link, group_slots, per_bin)
    grads = contrast(inbox[:, 0], inbox[:, 1], allowed, valid.astype(jnp.float32))
    returned = lax.all_to_all(
        grads.reshape(sources, per_owner, views, emb_dim),
        "dp",
        split_axis=0,
        concat_axis=0,
        tiled=True,
    )
    row_grads = returned.reshape(group_slots, views, emb_dim)[target].astype(jnp.float32)
    grad_rows = (
        scale * (row_grads - unit * jnp.sum(unit * row_grads, axis=2, keepdims=True))
    ).astype(jnp.bfloat16)
    column_start = lax.axis_index("bin") * part_rows
    trunk = lax.all_gather(features, "bin", axis=0, tiled=True)
    outgrad = lax.all_gather(grad_rows, "bin", axis=0, tiled=True)
    columns = lax.dynamic_slice_in_dim(trunk, column_start, part_rows, 2)
    count = trunk.shape[0]
    local_grad = lax.dot_general(
        columns.reshape(count * views, part_rows),
        outgrad.reshape(count * views, emb_dim),
        (((0,), (0,)), ((), ())),
        preferred_element_type=jnp.float32,
    )
    grad_weight = lax.psum_scatter(local_grad, "dp", scatter_dimension=0, tiled=True) / rows_dev
    return (grad_rows, grad_weight)


WIDTHS = (128, 256, 256, 256, 128)
CHUNKS = len(WIDTHS)
MESH = pl.DeviceIdType.MESH
F32 = jnp.float32
BF16 = jnp.bfloat16


def owners_kernel(
    n_dp, block, per_bin, rows_dev,
    feat, weight, row_bin, bin_owner, bin_link,
    out_rows, out_weight,
    wbuf, fcols, outbox, inbox, flag_out, flag_in, grads, returned, gathered,
    terms, terms16, from_x, pairs, pairs16, from_z,
    w_send, w_recv, f_send, f_recv, flag_send, flag_recv, a_send, a_recv,
    b_send, b_recv, g_send, g_recv, x_send, x_recv, z_send, z_recv,
):
    dp = lax.axis_index("dp")
    col = lax.axis_index("bin")
    half, core = col // 2, col % 2
    sib = half * 2 + (1 - core)
    peer = (1 - half) * 2 + core
    diag = (1 - half) * 2 + (1 - core)
    near = (col, sib, peer, diag)
    ahead = [lax.rem(dp + m, n_dp) for m in range(n_dp)]
    behind = [lax.rem(dp + n_dp - m, n_dp) for m in range(n_dp)]
    rows2, feat_dim = feat.shape
    part = weight.shape[0]
    emb = weight.shape[1]
    slots = n_dp * block
    piece = part // n_dp
    bins = bin_owner.shape[0]
    sends = []

    def push(src, dst, send, recv, device):
        copy = pltpu.make_async_remote_copy(
            src_ref=src, dst_ref=dst, send_sem=send, recv_sem=recv,
            device_id=device, device_id_type=MESH,
        )
        copy.start()
        sends.append(copy)
        return copy

    barrier = pltpu.get_barrier_semaphore()
    for other in near[1:]:
        pl.semaphore_signal(barrier, inc=1, device_id=(dp, other), device_id_type=MESH)
    for m in range(1, n_dp):
        pl.semaphore_signal(barrier, inc=1, device_id=(ahead[m], col), device_id_type=MESH)
    pl.semaphore_wait(barrier, 3 + n_dp - 1)

    lanes = [pl.ds(sum(WIDTHS[:k]), WIDTHS[k]) for k in range(CHUNKS)]
    own_w = []
    for k in range(CHUNKS):
        to_peer = push(
            weight.at[:, lanes[k]], wbuf.at[1, :, lanes[k]],
            w_send.at[1, k], w_recv.at[1, k], (dp, peer),
        )
        to_sib = push(
            weight.at[:, lanes[k]], wbuf.at[0, :, lanes[k]],
            w_send.at[0, k], w_recv.at[0, k], (dp, sib),
        )
        own_w.append((to_sib, to_peer))

    pos = lax.broadcasted_iota(jnp.int32, (rows_dev, rows2), 0)
    lane_row = lax.broadcasted_iota(jnp.int32, (rows_dev, rows2), 1) // 2
    bin_col = jnp.broadcast_to(row_bin[...], (rows_dev, rows2))
    bin_row = jnp.sum(jnp.where(pos == lane_row, bin_col, 0), axis=0, keepdims=True)
    seat = jnp.sum(
        jnp.where((bin_col == bin_row) & (pos < lane_row), 1, 0), axis=0, keepdims=True
    )
    target = seat
    link = jnp.int32(0)
    for b in range(bins):
        owner = bin_owner[b]
        local_bin = jnp.int32(0)
        for b2 in range(b):
            local_bin = local_bin + jnp.where(bin_owner[b2] == owner, 1, 0)
        away = owner - dp
        away = jnp.where(away < 0, away + n_dp, away)
        target = target + jnp.where(bin_row == b, away * block + local_bin * per_bin, 0)
        if b + 1 < bins:
            link = link + jnp.where((owner == dp) & (local_bin == 0), bin_link[b], 0)
    place = lax.broadcasted_iota(jnp.int32, (slots, rows2), 0)
    view = lax.broadcasted_iota(jnp.int32, (slots, rows2), 1) % 2
    here = place == jnp.broadcast_to(target, (slots, rows2))
    pick = [
        jnp.where(here & (view == v), 1.0, 0.0).astype(F32) for v in range(2)
    ]
    flags = jnp.broadcast_to(jnp.sum(pick[0], axis=1, keepdims=True), (slots, 128)).astype(BF16)
    pick = [p.astype(BF16) for p in pick]
    flag_out[...] = flags
    flag_in[0:block, :] = flags[0:block]
    flag_copies = []
    for m in range(1, n_dp):
        span = pl.ds(m * block, block)
        flag_copies.append(push(
            flag_out.at[span], flag_in.at[span], flag_send.at[m], flag_recv.at[m],
            (ahead[m], col),
        ))

    order = list(range(n_dp - 1, 0, -1))

    def start_out(k):
        copies = []
        for m in order:
            span = pl.ds(m * block, block)
            copies.append(push(
                outbox.at[:, span, lanes[k]], inbox.at[:, span, lanes[k]],
                a_send.at[k, m], a_recv.at[k, m], (ahead[m], col),
            ))
        return copies

    def columns_of(other):
        return pl.ds(pl.multiple_of(other * part, part), part)

    out_copies = []
    for k in range(CHUNKS):
        to_sib, to_peer = own_w[k]
        to_peer.wait_recv()
        relay = push(
            wbuf.at[1, :, lanes[k]], wbuf.at[2, :, lanes[k]],
            w_send.at[2, k], w_recv.at[2, k], (dp, sib),
        )
        y = jnp.dot(feat[:, columns_of(col)], weight[:, lanes[k]], preferred_element_type=F32)
        y += jnp.dot(feat[:, columns_of(peer)], wbuf[1, :, lanes[k]], preferred_element_type=F32)
        to_sib.wait_recv()
        y += jnp.dot(feat[:, columns_of(sib)], wbuf[0, :, lanes[k]], preferred_element_type=F32)
        relay.wait_recv()
        y += jnp.dot(feat[:, columns_of(diag)], wbuf[2, :, lanes[k]], preferred_element_type=F32)
        y = y.astype(BF16)
        for v in range(2):
            placed = jnp.dot(pick[v], y, preferred_element_type=F32).astype(BF16)
            outbox[v, :, lanes[k]] = placed
            inbox[v, 0:block, lanes[k]] = placed[0:block]
        out_copies.append(start_out(k))

    f_copies = []
    for x in (2, 3, 1):
        f_copies.append(push(
            feat.at[:, columns_of(near[x])], fcols.at[pl.ds(x * rows2, rows2), :],
            f_send.at[x], f_recv.at[x], (dp, near[x]),
        ))
    fcols[0:rows2, :] = feat[:, columns_of(col)]

    for copy in flag_copies:
        copy.wait_recv()
    raw = jnp.zeros((slots, slots), F32)
    square = [jnp.zeros((slots, 1), F32) for _ in range(2)]
    for k in range(CHUNKS):
        for copy in out_copies[k]:
            copy.wait_recv()
        raw += lax.dot_general(
            inbox[0, :, lanes[k]], inbox[1, :, lanes[k]], (((1,), (1,)), ((), ())), preferred_element_type=F32
        )
        for v in range(2):
            row = inbox[v, :, lanes[k]].astype(F32)
            square[v] += jnp.sum(row * row, axis=1, keepdims=True)
    scale0 = lax.rsqrt(square[0] + 1e-06)
    scale1 = lax.rsqrt(square[1] + 1e-06)
    s_pos = lax.broadcasted_iota(jnp.int32, (slots, slots), 0)
    t_pos = lax.broadcasted_iota(jnp.int32, (slots, slots), 1)
    eye = s_pos == t_pos
    scale1_row = jnp.sum(jnp.where(eye, scale1, 0.0), axis=0, keepdims=True)
    valid = flag_in[:, 0:1].astype(F32)
    valid_row = jnp.sum(jnp.where(eye, valid, 0.0), axis=0, keepdims=True)
    s_bin = (lax.broadcasted_iota(jnp.int32, (slots, 1), 0) % block >= per_bin).astype(jnp.int32)
    t_bin = (lax.broadcasted_iota(jnp.int32, (1, slots), 1) % block >= per_bin).astype(jnp.int32)
    bound = jnp.where(s_bin == t_bin, 1.0, (link == 1).astype(F32))
    allowed = jnp.where(eye, 1.0, valid * valid_row * bound)
    scores = raw * scale0 * scale1_row / SOFTMAX_TEMP_SCALE
    weights = allowed * jnp.exp(scores)
    shares = weights / jnp.sum(weights, axis=1, keepdims=True)
    logit = ((shares - jnp.where(eye, 1.0, 0.0)) * valid).astype(BF16).astype(F32)
    slope = logit * scores
    lean0 = jnp.sum(slope, axis=1, keepdims=True) * scale0 * scale0
    lean1_row = jnp.sum(slope, axis=0, keepdims=True) * scale1_row * scale1_row
    lean1 = jnp.sum(jnp.where(eye, lean1_row, 0.0), axis=1, keepdims=True)
    mix = logit * scale0 * scale1_row / SOFTMAX_TEMP_SCALE
    high = mix.astype(BF16)
    low = (mix - high.astype(F32)).astype(BF16)
    high_t, low_t = high.T, low.T

    back_copies = []
    for k in range(CHUNKS):
        y0, y1 = inbox[0, :, lanes[k]], inbox[1, :, lanes[k]]
        g0 = jnp.dot(high, y1, preferred_element_type=F32)
        g0 += jnp.dot(low, y1, preferred_element_type=F32) - lean0 * y0.astype(F32)
        g1 = jnp.dot(high_t, y0, preferred_element_type=F32)
        g1 += jnp.dot(low_t, y0, preferred_element_type=F32) - lean1 * y1.astype(F32)
        for v, g in ((0, g0.astype(BF16)), (1, g1.astype(BF16))):
            grads[v, :, lanes[k]] = g
            returned[v, 0:block, lanes[k]] = g[0:block]
        copies = []
        for m in order:
            span = pl.ds(m * block, block)
            copies.append(push(
                grads.at[:, span, lanes[k]], returned.at[:, span, lanes[k]],
                b_send.at[k, m], b_recv.at[k, m], (behind[m], col),
            ))
        back_copies.append(copies)

    for copy in f_copies:
        copy.wait_recv()
    across = (dp // 2) * 2 + (1 - dp % 2)
    layer, side = dp // 2, dp % 2
    layers = n_dp // 2
    x_copies, z_copies = [], []

    def finish_pair(k):
        x_copies[k].wait_recv()
        pair = terms[:, side, :, lanes[k]] + from_x[:, :, lanes[k]].astype(F32)
        pairs[:, :, lanes[k]] = pair
        pairs16[:, :, lanes[k]] = pair.astype(BF16)
        copies = []
        for step in range(layers - 1, 0, -1):
            to = lax.rem(layer + step, layers)
            copies.append(push(
                pairs16.at[to, :, lanes[k]], from_z.at[step, :, lanes[k]],
                z_send.at[k, step], z_recv.at[k, step], (to * 2 + side, col),
            ))
        z_copies.append(copies)

    for k in range(CHUNKS):
        for copy in back_copies[k]:
            copy.wait_recv()
        rows = jnp.zeros((rows2, WIDTHS[k]), F32)
        for v in range(2):
            rows += lax.dot_general(
                pick[v], returned[v, :, lanes[k]], (((0,), (0,)), ((), ())), preferred_element_type=F32
            )
        rows = rows.astype(BF16)
        out_rows[:, lanes[k]] = rows
        gathered[0:rows2, lanes[k]] = rows
        own = gathered.at[pl.ds(0, rows2), lanes[k]]
        spans = [pl.ds(x * rows2, rows2) for x in range(4)]
        to_peer = push(
            own, gathered.at[spans[2], lanes[k]], g_send.at[1, k], g_recv.at[1, k], (dp, peer)
        )
        to_sib = push(
            own, gathered.at[spans[1], lanes[k]], g_send.at[0, k], g_recv.at[0, k], (dp, sib)
        )
        if k > 0:
            finish_pair(k - 1)
        to_peer.wait_recv()
        relay = push(
            gathered.at[spans[2], lanes[k]], gathered.at[spans[3], lanes[k]],
            g_send.at[2, k], g_recv.at[2, k], (dp, sib),
        )
        to_sib.wait_recv()
        relay.wait_recv()
        term = lax.dot_general(
            fcols[...], gathered[:, lanes[k]], (((0,), (0,)), ((), ())), preferred_element_type=F32
        )
        term = term.reshape(layers, 2, piece, WIDTHS[k])
        terms[:, :, :, lanes[k]] = term
        terms16[:, :, :, lanes[k]] = term.astype(BF16)
        x_copies.append(push(
            terms16.at[:, 1 - side, :, lanes[k]], from_x.at[:, :, lanes[k]],
            x_send.at[k], x_recv.at[k], (across, col),
        ))
    finish_pair(CHUNKS - 1)
    for k in range(CHUNKS):
        total = pairs[layer, :, lanes[k]]
        for copy in z_copies[k]:
            copy.wait_recv()
        for step in range(1, layers):
            total += from_z[step, :, lanes[k]].astype(F32)
        out_weight[:, lanes[k]] = total / rows_dev
    for copy in sends:
        copy.wait_send()


def local_kernel(features, head_weight, bin_of_row, bin_owner, bin_link):
    rows_dev, views, feat_dim = features.shape
    part, emb = head_weight.shape
    n_dp = lax.axis_size("dp")
    bins = bin_owner.shape[0]
    per_bin = max(2, 2 * rows_dev // bins)
    block = -(-per_bin * MOSTB // 16) * 16
    slots = n_dp * block
    rows2 = rows_dev * views
    layers = n_dp // 2
    piece = part // n_dp
    vmem = pl.BlockSpec(memory_space=pltpu.VMEM)
    smem = pl.BlockSpec(memory_space=pltpu.SMEM)
    dma = pltpu.SemaphoreType.DMA
    wide = pltpu.VMEM((views, slots, emb), BF16)
    grad_rows, grad_weight = pl.pallas_call(
        functools.partial(owners_kernel, n_dp, block, per_bin, rows_dev),
        out_shape=(
            jax.ShapeDtypeStruct((rows2, emb), BF16),
            jax.ShapeDtypeStruct((piece, emb), F32),
        ),
        in_specs=[vmem, vmem, vmem, smem, smem],
        out_specs=(vmem, vmem),
        scratch_shapes=[
            pltpu.VMEM((3, part, emb), BF16),
            pltpu.VMEM((4 * rows2, part), BF16),
            wide, wide,
            pltpu.VMEM((slots, 128), BF16),
            pltpu.VMEM((slots, 128), BF16),
            wide, wide,
            pltpu.VMEM((4 * rows2, emb), BF16),
            pltpu.VMEM((layers, 2, piece, emb), F32),
            pltpu.VMEM((layers, 2, piece, emb), BF16),
            pltpu.VMEM((layers, piece, emb), BF16),
            pltpu.VMEM((layers, piece, emb), F32),
            pltpu.VMEM((layers, piece, emb), BF16),
            pltpu.VMEM((layers, piece, emb), BF16),
            dma((3, CHUNKS)), dma((3, CHUNKS)),
            dma((4,)), dma((4,)),
            dma((n_dp,)), dma((n_dp,)),
            dma((CHUNKS, n_dp)), dma((CHUNKS, n_dp)),
            dma((CHUNKS, n_dp)), dma((CHUNKS, n_dp)),
            dma((3, CHUNKS)), dma((3, CHUNKS)),
            dma((CHUNKS,)), dma((CHUNKS,)),
            dma((CHUNKS, layers)), dma((CHUNKS, layers)),
        ],
        compiler_params=pltpu.CompilerParams(
            collective_id=0, has_side_effects=True, vmem_limit_bytes=48 * 1024 * 1024
        ),
        cost_estimate=pl.CostEstimate(
            flops=4 * rows2 * feat_dim * emb, bytes_accessed=16 * 1024 * 1024, transcendentals=0
        ),
    )(features.reshape(rows2, feat_dim), head_weight, bin_of_row, bin_owner, bin_link)
    return grad_rows.reshape(rows_dev, views, emb), grad_weight


def solution(mesh):
    small = mesh.shape["dp"] <= 8 and mesh.shape["bin"] == 4
    return jax.shard_map(
        local_kernel if small else local,
        mesh=mesh,
        in_specs=(P(("dp", "bin"), None, None), P("bin", None), P(("dp", "bin"), None), P(), P()),
        out_specs=(P(("dp", "bin"), None, None), P(("bin", "dp"), None)),
        check_vma=False,
    )
```

```python
import functools

import jax
import jax.numpy as jnp
from jax import lax
from jax.experimental import pallas as pl
from jax.experimental.pallas import tpu as pltpu
from jax.sharding import PartitionSpec as P

MOSTB = 2


SOFTMAX_TEMP_SCALE = 0.1


def allowed_mask(valid, first, bin_link, group_slots, per_bin):
    per_owner = per_bin * MOSTB
    position = jnp.arange(group_slots, dtype=jnp.int32)
    local_bin = position % per_owner // per_bin
    padded = jnp.concatenate([bin_link, jnp.zeros((MOSTB,), jnp.int32)])
    nearby = lax.dynamic_slice(padded, (first,), (MOSTB,))
    lower = jnp.minimum(local_bin[:, None], local_bin[None, :])
    linked = jnp.zeros((group_slots, group_slots), jnp.int32)
    for height in range(MOSTB):
        linked = linked + jnp.where(lower == height, nearby[height], 0)
    spacing = jnp.abs(local_bin[:, None] - local_bin[None, :])
    paired = valid[:, None] & valid[None, :]
    allowed = paired & ((spacing == 0) | (spacing == 1) & (linked == 1))
    allowed = allowed | (position[:, None] == position[None, :])
    return allowed.astype(jnp.float32)


def contrast(query_rows, key_matrix, allowed, valid):
    similarity_scores = (
        lax.dot_general(
            query_rows, key_matrix, (((1,), (1,)), ((), ())), preferred_element_type=jnp.float32
        )
        / SOFTMAX_TEMP_SCALE
    )
    weights = allowed * jnp.exp(similarity_scores)
    shares = weights / jnp.sum(weights, axis=1, keepdims=True)
    position = jnp.arange(query_rows.shape[0], dtype=jnp.int32)
    diagonal = (position[:, None] == position[None, :]).astype(jnp.float32)
    logit_gradient = ((shares - diagonal) * valid[:, None]).astype(jnp.bfloat16)
    query_gradient = (
        jnp.dot(logit_gradient, key_matrix, preferred_element_type=jnp.float32) / SOFTMAX_TEMP_SCALE
    ).astype(jnp.bfloat16)
    key_gradient_rows = (
        lax.dot_general(
            logit_gradient, query_rows, (((0,), (0,)), ((), ())), preferred_element_type=jnp.float32
        )
        / SOFTMAX_TEMP_SCALE
    ).astype(jnp.bfloat16)
    return jnp.stack([query_gradient, key_gradient_rows], axis=1)


def local(features, head_weight, bin_of_row, bin_owner, bin_link):
    rows_dev, views, feat_dim = features.shape
    part_rows, emb_dim = head_weight.shape
    sources = lax.axis_size("dp")
    bin_count = bin_owner.shape[0]
    per_bin = max(2, 2 * rows_dev // bin_count)
    per_owner = per_bin * MOSTB
    group_slots = sources * per_owner
    flat = features.reshape(rows_dev * views, feat_dim)
    columns = flat
    folded = jnp.dot(
        columns,
        lax.all_gather(head_weight, "bin", axis=0, tiled=True),
        preferred_element_type=jnp.float32,
    )
    embedded = folded.reshape(rows_dev, views, emb_dim)
    scale = lax.rsqrt(jnp.sum(embedded * embedded, axis=2, keepdims=True) + 1e-06)
    unit = embedded * scale
    sent = unit.astype(jnp.bfloat16)
    row_bins = bin_of_row[:, 0]
    lookup = row_bins[:, None] == jnp.arange(bin_count, dtype=jnp.int32)[None, :]
    owner = jnp.sum(jnp.where(lookup, bin_owner[None, :], 0), axis=1)
    first_by_bin = jnp.sum((bin_owner[None, :] < bin_owner[:, None]).astype(jnp.int32), axis=1)
    local_bin = row_bins - jnp.sum(jnp.where(lookup, first_by_bin[None, :], 0), axis=1)
    order = jnp.arange(rows_dev, dtype=jnp.int32)
    earlier = (row_bins[:, None] == row_bins[None, :]) & (order[None, :] < order[:, None])
    seat = jnp.sum(earlier.astype(jnp.int32), axis=1)
    target = owner * per_owner + local_bin * per_bin + seat
    outbox = jnp.zeros((group_slots, views, emb_dim), jnp.bfloat16).at[target].set(sent)
    filled = (
        jnp.zeros((group_slots,), jnp.bfloat16).at[target].set(jnp.ones((rows_dev,), jnp.bfloat16))
    )
    inbox, present = (
        lax.all_to_all(
            outbox.reshape(sources, per_owner, views, emb_dim),
            "dp",
            split_axis=0,
            concat_axis=0,
            tiled=True,
        ),
        lax.all_to_all(
            filled.reshape(sources, per_owner), "dp", split_axis=0, concat_axis=0, tiled=True
        ),
    )
    inbox = inbox.reshape(group_slots, views, emb_dim)
    valid = present.reshape(group_slots) > 0.5
    first = jnp.sum((bin_owner < lax.axis_index("dp")).astype(jnp.int32))
    allowed = allowed_mask(valid, first, bin_link, group_slots, per_bin)
    grads = contrast(inbox[:, 0], inbox[:, 1], allowed, valid.astype(jnp.float32))
    returned = lax.all_to_all(
        grads.reshape(sources, per_owner, views, emb_dim),
        "dp",
        split_axis=0,
        concat_axis=0,
        tiled=True,
    )
    row_grads = returned.reshape(group_slots, views, emb_dim)[target].astype(jnp.float32)
    grad_rows = (
        scale * (row_grads - unit * jnp.sum(unit * row_grads, axis=2, keepdims=True))
    ).astype(jnp.bfloat16)
    column_start = lax.axis_index("bin") * part_rows
    trunk = lax.all_gather(features, "bin", axis=0, tiled=True)
    outgrad = lax.all_gather(grad_rows, "bin", axis=0, tiled=True)
    columns = lax.dynamic_slice_in_dim(trunk, column_start, part_rows, 2)
    count = trunk.shape[0]
    local_grad = lax.dot_general(
        columns.reshape(count * views, part_rows),
        outgrad.reshape(count * views, emb_dim),
        (((0,), (0,)), ((), ())),
        preferred_element_type=jnp.float32,
    )
    grad_weight = lax.psum_scatter(local_grad, "dp", scatter_dimension=0, tiled=True) / rows_dev
    return (grad_rows, grad_weight)


WIDTHS = (128, 256, 256, 256, 128)
CHUNKS = len(WIDTHS)
AHEAD = 2
MESH = pl.DeviceIdType.MESH
F32 = jnp.float32
BF16 = jnp.bfloat16


def owners_kernel(
    n_dp, block, per_bin, rows_dev,
    feat, weight, row_bin, bin_owner, bin_link,
    out_rows, out_weight,
    wbuf, fcols, outbox, inbox, flag_out, flag_in, grads, returned, gathered,
    terms, terms16, from_x, pairs, pairs16, from_z,
    w_send, w_recv, f_send, f_recv, flag_send, flag_recv, a_send, a_recv,
    b_send, b_recv, g_send, g_recv, x_send, x_recv, z_send, z_recv,
):
    dp = lax.axis_index("dp")
    col = lax.axis_index("bin")
    half, core = col // 2, col % 2
    sib = half * 2 + (1 - core)
    peer = (1 - half) * 2 + core
    diag = (1 - half) * 2 + (1 - core)
    near = (col, sib, peer, diag)
    ahead = [lax.rem(dp + m, n_dp) for m in range(n_dp)]
    behind = [lax.rem(dp + n_dp - m, n_dp) for m in range(n_dp)]
    rows2, feat_dim = feat.shape
    part = weight.shape[0]
    emb = weight.shape[1]
    slots = n_dp * block
    piece = part // n_dp
    bins = bin_owner.shape[0]
    sends = []

    def push(src, dst, send, recv, device):
        copy = pltpu.make_async_remote_copy(
            src_ref=src, dst_ref=dst, send_sem=send, recv_sem=recv,
            device_id=device, device_id_type=MESH,
        )
        copy.start()
        sends.append(copy)
        return copy

    barrier = pltpu.get_barrier_semaphore()
    for other in near[1:]:
        pl.semaphore_signal(barrier, inc=1, device_id=(dp, other), device_id_type=MESH)
    for m in range(1, n_dp):
        pl.semaphore_signal(barrier, inc=1, device_id=(ahead[m], col), device_id_type=MESH)
    pl.semaphore_wait(barrier, 3 + n_dp - 1)

    lanes = [pl.ds(sum(WIDTHS[:k]), WIDTHS[k]) for k in range(CHUNKS)]
    own_w = []

    def start_weight(k):
        to_peer = push(
            weight.at[:, lanes[k]], wbuf.at[1, :, lanes[k]],
            w_send.at[1, k], w_recv.at[1, k], (dp, peer),
        )
        to_sib = push(
            weight.at[:, lanes[k]], wbuf.at[0, :, lanes[k]],
            w_send.at[0, k], w_recv.at[0, k], (dp, sib),
        )
        own_w.append((to_sib, to_peer))

    for k in range(AHEAD):
        start_weight(k)

    pos = lax.broadcasted_iota(jnp.int32, (rows_dev, rows2), 0)
    lane_row = lax.broadcasted_iota(jnp.int32, (rows_dev, rows2), 1) // 2
    bin_col = jnp.broadcast_to(row_bin[...], (rows_dev, rows2))
    bin_row = jnp.sum(jnp.where(pos == lane_row, bin_col, 0), axis=0, keepdims=True)
    seat = jnp.sum(
        jnp.where((bin_col == bin_row) & (pos < lane_row), 1, 0), axis=0, keepdims=True
    )
    target = seat
    link = jnp.int32(0)
    for b in range(bins):
        owner = bin_owner[b]
        local_bin = jnp.int32(0)
        for b2 in range(b):
            local_bin = local_bin + jnp.where(bin_owner[b2] == owner, 1, 0)
        away = owner - dp
        away = jnp.where(away < 0, away + n_dp, away)
        target = target + jnp.where(bin_row == b, away * block + local_bin * per_bin, 0)
        if b + 1 < bins:
            link = link + jnp.where((owner == dp) & (local_bin == 0), bin_link[b], 0)
    place = lax.broadcasted_iota(jnp.int32, (slots, rows2), 0)
    view = lax.broadcasted_iota(jnp.int32, (slots, rows2), 1) % 2
    here = place == jnp.broadcast_to(target, (slots, rows2))
    pick = [
        jnp.where(here & (view == v), 1.0, 0.0).astype(F32) for v in range(2)
    ]
    flags = jnp.broadcast_to(jnp.sum(pick[0], axis=1, keepdims=True), (slots, 128)).astype(BF16)
    pick = [p.astype(BF16) for p in pick]
    flag_out[...] = flags
    flag_in[0:block, :] = flags[0:block]
    flag_copies = []
    for m in range(1, n_dp):
        span = pl.ds(m * block, block)
        flag_copies.append(push(
            flag_out.at[span], flag_in.at[span], flag_send.at[m], flag_recv.at[m],
            (ahead[m], col),
        ))

    order = list(range(n_dp - 1, 0, -1))

    def start_out(k):
        copies = []
        for m in order:
            span = pl.ds(m * block, block)
            copies.append(push(
                outbox.at[:, span, lanes[k]], inbox.at[:, span, lanes[k]],
                a_send.at[k, m], a_recv.at[k, m], (ahead[m], col),
            ))
        return copies

    def columns_of(other):
        return pl.ds(pl.multiple_of(other * part, part), part)

    out_copies = []
    for k in range(CHUNKS):
        to_sib, to_peer = own_w[k]
        to_peer.wait_recv()
        if k + AHEAD < CHUNKS:
            start_weight(k + AHEAD)
        relay = push(
            wbuf.at[1, :, lanes[k]], wbuf.at[2, :, lanes[k]],
            w_send.at[2, k], w_recv.at[2, k], (dp, sib),
        )
        y = jnp.dot(feat[:, columns_of(col)], weight[:, lanes[k]], preferred_element_type=F32)
        y += jnp.dot(feat[:, columns_of(peer)], wbuf[1, :, lanes[k]], preferred_element_type=F32)
        to_sib.wait_recv()
        y += jnp.dot(feat[:, columns_of(sib)], wbuf[0, :, lanes[k]], preferred_element_type=F32)
        relay.wait_recv()
        y += jnp.dot(feat[:, columns_of(diag)], wbuf[2, :, lanes[k]], preferred_element_type=F32)
        y = y.astype(BF16)
        for v in range(2):
            placed = jnp.dot(pick[v], y, preferred_element_type=F32).astype(BF16)
            outbox[v, :, lanes[k]] = placed
            inbox[v, 0:block, lanes[k]] = placed[0:block]
        out_copies.append(start_out(k))

    f_copies = []
    for x in (2, 3, 1):
        f_copies.append(push(
            feat.at[:, columns_of(near[x])], fcols.at[pl.ds(x * rows2, rows2), :],
            f_send.at[x], f_recv.at[x], (dp, near[x]),
        ))
    fcols[0:rows2, :] = feat[:, columns_of(col)]

    for copy in flag_copies:
        copy.wait_recv()
    raw = jnp.zeros((slots, slots), F32)
    square = [jnp.zeros((slots, 1), F32) for _ in range(2)]
    for k in range(CHUNKS):
        for copy in out_copies[k]:
            copy.wait_recv()
        raw += lax.dot_general(
            inbox[0, :, lanes[k]], inbox[1, :, lanes[k]], (((1,), (1,)), ((), ())), preferred_element_type=F32
        )
        for v in range(2):
            row = inbox[v, :, lanes[k]].astype(F32)
            square[v] += jnp.sum(row * row, axis=1, keepdims=True)
    scale0 = lax.rsqrt(square[0] + 1e-06)
    scale1 = lax.rsqrt(square[1] + 1e-06)
    s_pos = lax.broadcasted_iota(jnp.int32, (slots, slots), 0)
    t_pos = lax.broadcasted_iota(jnp.int32, (slots, slots), 1)
    eye = s_pos == t_pos
    scale1_row = jnp.sum(jnp.where(eye, scale1, 0.0), axis=0, keepdims=True)
    valid = flag_in[:, 0:1].astype(F32)
    valid_row = jnp.sum(jnp.where(eye, valid, 0.0), axis=0, keepdims=True)
    s_bin = (lax.broadcasted_iota(jnp.int32, (slots, 1), 0) % block >= per_bin).astype(jnp.int32)
    t_bin = (lax.broadcasted_iota(jnp.int32, (1, slots), 1) % block >= per_bin).astype(jnp.int32)
    bound = jnp.where(s_bin == t_bin, 1.0, (link == 1).astype(F32))
    allowed = jnp.where(eye, 1.0, valid * valid_row * bound)
    scores = raw * scale0 * scale1_row / SOFTMAX_TEMP_SCALE
    weights = allowed * jnp.exp(scores)
    shares = weights / jnp.sum(weights, axis=1, keepdims=True)
    logit = ((shares - jnp.where(eye, 1.0, 0.0)) * valid).astype(BF16).astype(F32)
    slope = logit * scores
    lean0 = jnp.sum(slope, axis=1, keepdims=True) * scale0 * scale0
    lean1_row = jnp.sum(slope, axis=0, keepdims=True) * scale1_row * scale1_row
    lean1 = jnp.sum(jnp.where(eye, lean1_row, 0.0), axis=1, keepdims=True)
    mix = logit * scale0 * scale1_row / SOFTMAX_TEMP_SCALE
    high = mix.astype(BF16)
    low = (mix - high.astype(F32)).astype(BF16)
    high_t, low_t = high.T, low.T

    back_copies = []

    def start_back(k):
        y0, y1 = inbox[0, :, lanes[k]], inbox[1, :, lanes[k]]
        g0 = jnp.dot(high, y1, preferred_element_type=F32)
        g0 += jnp.dot(low, y1, preferred_element_type=F32) - lean0 * y0.astype(F32)
        g1 = jnp.dot(high_t, y0, preferred_element_type=F32)
        g1 += jnp.dot(low_t, y0, preferred_element_type=F32) - lean1 * y1.astype(F32)
        for v, g in ((0, g0.astype(BF16)), (1, g1.astype(BF16))):
            grads[v, :, lanes[k]] = g
            returned[v, 0:block, lanes[k]] = g[0:block]
        copies = []
        for m in order:
            span = pl.ds(m * block, block)
            copies.append(push(
                grads.at[:, span, lanes[k]], returned.at[:, span, lanes[k]],
                b_send.at[k, m], b_recv.at[k, m], (behind[m], col),
            ))
        back_copies.append(copies)

    for k in range(AHEAD):
        start_back(k)

    for copy in f_copies:
        copy.wait_recv()
    across = (dp // 2) * 2 + (1 - dp % 2)
    layer, side = dp // 2, dp % 2
    layers = n_dp // 2
    x_copies, z_copies = [], []

    def finish_pair(k):
        x_copies[k].wait_recv()
        pair = terms[:, side, :, lanes[k]] + from_x[:, :, lanes[k]].astype(F32)
        pairs[:, :, lanes[k]] = pair
        pairs16[:, :, lanes[k]] = pair.astype(BF16)
        copies = []
        for step in range(layers - 1, 0, -1):
            to = lax.rem(layer + step, layers)
            copies.append(push(
                pairs16.at[to, :, lanes[k]], from_z.at[step, :, lanes[k]],
                z_send.at[k, step], z_recv.at[k, step], (to * 2 + side, col),
            ))
        z_copies.append(copies)

    for k in range(CHUNKS):
        for copy in back_copies[k]:
            copy.wait_recv()
        if k + AHEAD < CHUNKS:
            start_back(k + AHEAD)
        rows = jnp.zeros((rows2, WIDTHS[k]), F32)
        for v in range(2):
            rows += lax.dot_general(
                pick[v], returned[v, :, lanes[k]], (((0,), (0,)), ((), ())), preferred_element_type=F32
            )
        rows = rows.astype(BF16)
        out_rows[:, lanes[k]] = rows
        gathered[0:rows2, lanes[k]] = rows
        own = gathered.at[pl.ds(0, rows2), lanes[k]]
        spans = [pl.ds(x * rows2, rows2) for x in range(4)]
        to_peer = push(
            own, gathered.at[spans[2], lanes[k]], g_send.at[1, k], g_recv.at[1, k], (dp, peer)
        )
        to_sib = push(
            own, gathered.at[spans[1], lanes[k]], g_send.at[0, k], g_recv.at[0, k], (dp, sib)
        )
        if k > 0:
            finish_pair(k - 1)
        to_peer.wait_recv()
        relay = push(
            gathered.at[spans[2], lanes[k]], gathered.at[spans[3], lanes[k]],
            g_send.at[2, k], g_recv.at[2, k], (dp, sib),
        )
        to_sib.wait_recv()
        relay.wait_recv()
        term = lax.dot_general(
            fcols[...], gathered[:, lanes[k]], (((0,), (0,)), ((), ())), preferred_element_type=F32
        )
        term = term.reshape(layers, 2, piece, WIDTHS[k])
        terms[:, :, :, lanes[k]] = term
        terms16[:, :, :, lanes[k]] = term.astype(BF16)
        x_copies.append(push(
            terms16.at[:, 1 - side, :, lanes[k]], from_x.at[:, :, lanes[k]],
            x_send.at[k], x_recv.at[k], (across, col),
        ))
    finish_pair(CHUNKS - 1)
    for k in range(CHUNKS):
        total = pairs[layer, :, lanes[k]]
        for copy in z_copies[k]:
            copy.wait_recv()
        for step in range(1, layers):
            total += from_z[step, :, lanes[k]].astype(F32)
        out_weight[:, lanes[k]] = total / rows_dev
    for copy in sends:
        copy.wait_send()


def local_kernel(features, head_weight, bin_of_row, bin_owner, bin_link):
    rows_dev, views, feat_dim = features.shape
    part, emb = head_weight.shape
    n_dp = lax.axis_size("dp")
    bins = bin_owner.shape[0]
    per_bin = max(2, 2 * rows_dev // bins)
    block = -(-per_bin * MOSTB // 16) * 16
    slots = n_dp * block
    rows2 = rows_dev * views
    layers = n_dp // 2
    piece = part // n_dp
    vmem = pl.BlockSpec(memory_space=pltpu.VMEM)
    smem = pl.BlockSpec(memory_space=pltpu.SMEM)
    dma = pltpu.SemaphoreType.DMA
    wide = pltpu.VMEM((views, slots, emb), BF16)
    grad_rows, grad_weight = pl.pallas_call(
        functools.partial(owners_kernel, n_dp, block, per_bin, rows_dev),
        out_shape=(
            jax.ShapeDtypeStruct((rows2, emb), BF16),
            jax.ShapeDtypeStruct((piece, emb), F32),
        ),
        in_specs=[vmem, vmem, vmem, smem, smem],
        out_specs=(vmem, vmem),
        scratch_shapes=[
            pltpu.VMEM((3, part, emb), BF16),
            pltpu.VMEM((4 * rows2, part), BF16),
            wide, wide,
            pltpu.VMEM((slots, 128), BF16),
            pltpu.VMEM((slots, 128), BF16),
            wide, wide,
            pltpu.VMEM((4 * rows2, emb), BF16),
            pltpu.VMEM((layers, 2, piece, emb), F32),
            pltpu.VMEM((layers, 2, piece, emb), BF16),
            pltpu.VMEM((layers, piece, emb), BF16),
            pltpu.VMEM((layers, piece, emb), F32),
            pltpu.VMEM((layers, piece, emb), BF16),
            pltpu.VMEM((layers, piece, emb), BF16),
            dma((3, CHUNKS)), dma((3, CHUNKS)),
            dma((4,)), dma((4,)),
            dma((n_dp,)), dma((n_dp,)),
            dma((CHUNKS, n_dp)), dma((CHUNKS, n_dp)),
            dma((CHUNKS, n_dp)), dma((CHUNKS, n_dp)),
            dma((3, CHUNKS)), dma((3, CHUNKS)),
            dma((CHUNKS,)), dma((CHUNKS,)),
            dma((CHUNKS, layers)), dma((CHUNKS, layers)),
        ],
        compiler_params=pltpu.CompilerParams(
            collective_id=0, has_side_effects=True, vmem_limit_bytes=48 * 1024 * 1024
        ),
        cost_estimate=pl.CostEstimate(
            flops=4 * rows2 * feat_dim * emb, bytes_accessed=16 * 1024 * 1024, transcendentals=0
        ),
    )(features.reshape(rows2, feat_dim), head_weight, bin_of_row, bin_owner, bin_link)
    return grad_rows.reshape(rows_dev, views, emb), grad_weight


def solution(mesh):
    small = mesh.shape["dp"] <= 8 and mesh.shape["bin"] == 4
    return jax.shard_map(
        local_kernel if small else local,
        mesh=mesh,
        in_specs=(P(("dp", "bin"), None, None), P("bin", None), P(("dp", "bin"), None), P(), P()),
        out_specs=(P(("dp", "bin"), None, None), P(("bin", "dp"), None)),
        check_vma=False,
    )
```

```python
import functools

import jax
import jax.numpy as jnp
from jax import lax
from jax.experimental import pallas as pl
from jax.experimental.pallas import tpu as pltpu
from jax.sharding import PartitionSpec as P

MOSTB = 2


SOFTMAX_TEMP_SCALE = 0.1


def allowed_mask(valid, first, bin_link, group_slots, per_bin):
    per_owner = per_bin * MOSTB
    position = jnp.arange(group_slots, dtype=jnp.int32)
    local_bin = position % per_owner // per_bin
    padded = jnp.concatenate([bin_link, jnp.zeros((MOSTB,), jnp.int32)])
    nearby = lax.dynamic_slice(padded, (first,), (MOSTB,))
    lower = jnp.minimum(local_bin[:, None], local_bin[None, :])
    linked = jnp.zeros((group_slots, group_slots), jnp.int32)
    for height in range(MOSTB):
        linked = linked + jnp.where(lower == height, nearby[height], 0)
    spacing = jnp.abs(local_bin[:, None] - local_bin[None, :])
    paired = valid[:, None] & valid[None, :]
    allowed = paired & ((spacing == 0) | (spacing == 1) & (linked == 1))
    allowed = allowed | (position[:, None] == position[None, :])
    return allowed.astype(jnp.float32)


def contrast(query_rows, key_matrix, allowed, valid):
    similarity_scores = (
        lax.dot_general(
            query_rows, key_matrix, (((1,), (1,)), ((), ())), preferred_element_type=jnp.float32
        )
        / SOFTMAX_TEMP_SCALE
    )
    weights = allowed * jnp.exp(similarity_scores)
    shares = weights / jnp.sum(weights, axis=1, keepdims=True)
    position = jnp.arange(query_rows.shape[0], dtype=jnp.int32)
    diagonal = (position[:, None] == position[None, :]).astype(jnp.float32)
    logit_gradient = ((shares - diagonal) * valid[:, None]).astype(jnp.bfloat16)
    query_gradient = (
        jnp.dot(logit_gradient, key_matrix, preferred_element_type=jnp.float32) / SOFTMAX_TEMP_SCALE
    ).astype(jnp.bfloat16)
    key_gradient_rows = (
        lax.dot_general(
            logit_gradient, query_rows, (((0,), (0,)), ((), ())), preferred_element_type=jnp.float32
        )
        / SOFTMAX_TEMP_SCALE
    ).astype(jnp.bfloat16)
    return jnp.stack([query_gradient, key_gradient_rows], axis=1)


def local(features, head_weight, bin_of_row, bin_owner, bin_link):
    rows_dev, views, feat_dim = features.shape
    part_rows, emb_dim = head_weight.shape
    sources = lax.axis_size("dp")
    bin_count = bin_owner.shape[0]
    per_bin = max(2, 2 * rows_dev // bin_count)
    per_owner = per_bin * MOSTB
    group_slots = sources * per_owner
    flat = features.reshape(rows_dev * views, feat_dim)
    columns = flat
    folded = jnp.dot(
        columns,
        lax.all_gather(head_weight, "bin", axis=0, tiled=True),
        preferred_element_type=jnp.float32,
    )
    embedded = folded.reshape(rows_dev, views, emb_dim)
    scale = lax.rsqrt(jnp.sum(embedded * embedded, axis=2, keepdims=True) + 1e-06)
    unit = embedded * scale
    sent = unit.astype(jnp.bfloat16)
    row_bins = bin_of_row[:, 0]
    lookup = row_bins[:, None] == jnp.arange(bin_count, dtype=jnp.int32)[None, :]
    owner = jnp.sum(jnp.where(lookup, bin_owner[None, :], 0), axis=1)
    first_by_bin = jnp.sum((bin_owner[None, :] < bin_owner[:, None]).astype(jnp.int32), axis=1)
    local_bin = row_bins - jnp.sum(jnp.where(lookup, first_by_bin[None, :], 0), axis=1)
    order = jnp.arange(rows_dev, dtype=jnp.int32)
    earlier = (row_bins[:, None] == row_bins[None, :]) & (order[None, :] < order[:, None])
    seat = jnp.sum(earlier.astype(jnp.int32), axis=1)
    target = owner * per_owner + local_bin * per_bin + seat
    outbox = jnp.zeros((group_slots, views, emb_dim), jnp.bfloat16).at[target].set(sent)
    filled = (
        jnp.zeros((group_slots,), jnp.bfloat16).at[target].set(jnp.ones((rows_dev,), jnp.bfloat16))
    )
    inbox, present = (
        lax.all_to_all(
            outbox.reshape(sources, per_owner, views, emb_dim),
            "dp",
            split_axis=0,
            concat_axis=0,
            tiled=True,
        ),
        lax.all_to_all(
            filled.reshape(sources, per_owner), "dp", split_axis=0, concat_axis=0, tiled=True
        ),
    )
    inbox = inbox.reshape(group_slots, views, emb_dim)
    valid = present.reshape(group_slots) > 0.5
    first = jnp.sum((bin_owner < lax.axis_index("dp")).astype(jnp.int32))
    allowed = allowed_mask(valid, first, bin_link, group_slots, per_bin)
    grads = contrast(inbox[:, 0], inbox[:, 1], allowed, valid.astype(jnp.float32))
    returned = lax.all_to_all(
        grads.reshape(sources, per_owner, views, emb_dim),
        "dp",
        split_axis=0,
        concat_axis=0,
        tiled=True,
    )
    row_grads = returned.reshape(group_slots, views, emb_dim)[target].astype(jnp.float32)
    grad_rows = (
        scale * (row_grads - unit * jnp.sum(unit * row_grads, axis=2, keepdims=True))
    ).astype(jnp.bfloat16)
    column_start = lax.axis_index("bin") * part_rows
    trunk = lax.all_gather(features, "bin", axis=0, tiled=True)
    outgrad = lax.all_gather(grad_rows, "bin", axis=0, tiled=True)
    columns = lax.dynamic_slice_in_dim(trunk, column_start, part_rows, 2)
    count = trunk.shape[0]
    local_grad = lax.dot_general(
        columns.reshape(count * views, part_rows),
        outgrad.reshape(count * views, emb_dim),
        (((0,), (0,)), ((), ())),
        preferred_element_type=jnp.float32,
    )
    grad_weight = lax.psum_scatter(local_grad, "dp", scatter_dimension=0, tiled=True) / rows_dev
    return (grad_rows, grad_weight)


WIDTHS = (128, 256, 256, 256, 128)
CHUNKS = len(WIDTHS)
MESH = pl.DeviceIdType.MESH
F32 = jnp.float32
BF16 = jnp.bfloat16


def owners_kernel(
    n_dp, block, per_bin, rows_dev,
    feat, weight, row_bin, bin_owner, bin_link,
    out_rows, out_weight,
    wbuf, fcols, fcols_t, outbox, inbox, flag_out, flag_in, grads, returned, gathered,
    terms, terms16, from_x, pairs, pairs16, from_z,
    w_send, w_recv, f_send, f_recv, flag_send, flag_recv, a_send, a_recv,
    b_send, b_recv, g_send, g_recv, x_send, x_recv, z_send, z_recv,
):
    dp = lax.axis_index("dp")
    col = lax.axis_index("bin")
    half, core = col // 2, col % 2
    sib = half * 2 + (1 - core)
    peer = (1 - half) * 2 + core
    diag = (1 - half) * 2 + (1 - core)
    near = (col, sib, peer, diag)
    ahead = [lax.rem(dp + m, n_dp) for m in range(n_dp)]
    behind = [lax.rem(dp + n_dp - m, n_dp) for m in range(n_dp)]
    rows2, feat_dim = feat.shape
    part = weight.shape[0]
    emb = weight.shape[1]
    slots = n_dp * block
    piece = part // n_dp
    bins = bin_owner.shape[0]
    sends = []

    def push(src, dst, send, recv, device):
        copy = pltpu.make_async_remote_copy(
            src_ref=src, dst_ref=dst, send_sem=send, recv_sem=recv,
            device_id=device, device_id_type=MESH,
        )
        copy.start()
        sends.append(copy)
        return copy

    barrier = pltpu.get_barrier_semaphore()
    for other in near[1:]:
        pl.semaphore_signal(barrier, inc=1, device_id=(dp, other), device_id_type=MESH)
    for m in range(1, n_dp):
        pl.semaphore_signal(barrier, inc=1, device_id=(ahead[m], col), device_id_type=MESH)
    pl.semaphore_wait(barrier, 3 + n_dp - 1)

    lanes = [pl.ds(sum(WIDTHS[:k]), WIDTHS[k]) for k in range(CHUNKS)]
    own_w = []
    for k in range(CHUNKS):
        to_peer = push(
            weight.at[:, lanes[k]], wbuf.at[1, :, lanes[k]],
            w_send.at[1, k], w_recv.at[1, k], (dp, peer),
        )
        to_sib = push(
            weight.at[:, lanes[k]], wbuf.at[0, :, lanes[k]],
            w_send.at[0, k], w_recv.at[0, k], (dp, sib),
        )
        own_w.append((to_sib, to_peer))

    pos = lax.broadcasted_iota(jnp.int32, (rows_dev, rows2), 0)
    lane_row = lax.broadcasted_iota(jnp.int32, (rows_dev, rows2), 1) // 2
    bin_col = jnp.broadcast_to(row_bin[...], (rows_dev, rows2))
    bin_row = jnp.sum(jnp.where(pos == lane_row, bin_col, 0), axis=0, keepdims=True)
    seat = jnp.sum(
        jnp.where((bin_col == bin_row) & (pos < lane_row), 1, 0), axis=0, keepdims=True
    )
    target = seat
    link = jnp.int32(0)
    for b in range(bins):
        owner = bin_owner[b]
        local_bin = jnp.int32(0)
        for b2 in range(b):
            local_bin = local_bin + jnp.where(bin_owner[b2] == owner, 1, 0)
        away = owner - dp
        away = jnp.where(away < 0, away + n_dp, away)
        target = target + jnp.where(bin_row == b, away * block + local_bin * per_bin, 0)
        if b + 1 < bins:
            link = link + jnp.where((owner == dp) & (local_bin == 0), bin_link[b], 0)
    place = lax.broadcasted_iota(jnp.int32, (slots, rows2), 0)
    view = lax.broadcasted_iota(jnp.int32, (slots, rows2), 1) % 2
    here = place == jnp.broadcast_to(target, (slots, rows2))
    pick = [
        jnp.where(here & (view == v), 1.0, 0.0).astype(F32) for v in range(2)
    ]
    flags = jnp.broadcast_to(jnp.sum(pick[0], axis=1, keepdims=True), (slots, 128)).astype(BF16)
    pick_t = [p.T.astype(BF16) for p in pick]
    pick = [p.astype(BF16) for p in pick]
    flag_out[...] = flags
    flag_in[0:block, :] = flags[0:block]
    flag_copies = []
    for m in range(1, n_dp):
        span = pl.ds(m * block, block)
        flag_copies.append(push(
            flag_out.at[span], flag_in.at[span], flag_send.at[m], flag_recv.at[m],
            (ahead[m], col),
        ))

    order = list(range(n_dp - 1, 0, -1))

    def start_out(k):
        copies = []
        for m in order:
            span = pl.ds(m * block, block)
            copies.append(push(
                outbox.at[:, span, lanes[k]], inbox.at[:, span, lanes[k]],
                a_send.at[k, m], a_recv.at[k, m], (ahead[m], col),
            ))
        return copies

    def columns_of(other):
        return pl.ds(pl.multiple_of(other * part, part), part)

    out_copies = []
    for k in range(CHUNKS):
        to_sib, to_peer = own_w[k]
        to_peer.wait_recv()
        relay = push(
            wbuf.at[1, :, lanes[k]], wbuf.at[2, :, lanes[k]],
            w_send.at[2, k], w_recv.at[2, k], (dp, sib),
        )
        y = jnp.dot(feat[:, columns_of(col)], weight[:, lanes[k]], preferred_element_type=F32)
        y += jnp.dot(feat[:, columns_of(peer)], wbuf[1, :, lanes[k]], preferred_element_type=F32)
        to_sib.wait_recv()
        y += jnp.dot(feat[:, columns_of(sib)], wbuf[0, :, lanes[k]], preferred_element_type=F32)
        relay.wait_recv()
        y += jnp.dot(feat[:, columns_of(diag)], wbuf[2, :, lanes[k]], preferred_element_type=F32)
        y = y.astype(BF16)
        for v in range(2):
            placed = jnp.dot(pick[v], y, preferred_element_type=F32).astype(BF16)
            outbox[v, :, lanes[k]] = placed
            inbox[v, 0:block, lanes[k]] = placed[0:block]
        out_copies.append(start_out(k))

    f_copies = []
    for x in (2, 3, 1):
        f_copies.append(push(
            feat.at[:, columns_of(near[x])], fcols.at[pl.ds(x * rows2, rows2), :],
            f_send.at[x], f_recv.at[x], (dp, near[x]),
        ))
    fcols[0:rows2, :] = feat[:, columns_of(col)]

    for copy in flag_copies:
        copy.wait_recv()
    s_pos = lax.broadcasted_iota(jnp.int32, (slots, slots), 0)
    t_pos = lax.broadcasted_iota(jnp.int32, (slots, slots), 1)
    eye = s_pos == t_pos
    valid = flag_in[:, 0:1].astype(F32)
    valid_row = jnp.sum(jnp.where(eye, valid, 0.0), axis=0, keepdims=True)
    s_bin = (lax.broadcasted_iota(jnp.int32, (slots, 1), 0) % block >= per_bin).astype(jnp.int32)
    t_bin = (lax.broadcasted_iota(jnp.int32, (1, slots), 1) % block >= per_bin).astype(jnp.int32)
    bound = jnp.where(s_bin == t_bin, 1.0, (link == 1).astype(F32))
    allowed = jnp.where(eye, 1.0, valid * valid_row * bound)

    def turn_columns(x):
        span = pl.ds(x * rows2, rows2)
        fcols_t[:, span] = fcols[span, :].T

    turn_columns(0)
    raw = jnp.zeros((slots, slots), F32)
    square = [jnp.zeros((slots, 1), F32) for _ in range(2)]
    for k in range(CHUNKS):
        for copy in out_copies[k]:
            copy.wait_recv()
        raw += lax.dot_general(
            inbox[0, :, lanes[k]], inbox[1, :, lanes[k]], (((1,), (1,)), ((), ())), preferred_element_type=F32
        )
        for v in range(2):
            row = inbox[v, :, lanes[k]].astype(F32)
            square[v] += jnp.sum(row * row, axis=1, keepdims=True)
    scale0 = lax.rsqrt(square[0] + 1e-06)
    scale1 = lax.rsqrt(square[1] + 1e-06)
    scale1_row = jnp.sum(jnp.where(eye, scale1, 0.0), axis=0, keepdims=True)
    warm_row = scale1_row * (1.0 / SOFTMAX_TEMP_SCALE)
    scores = raw * scale0 * warm_row
    weights = allowed * jnp.exp(scores)
    shares = weights / jnp.sum(weights, axis=1, keepdims=True)
    logit = ((shares - jnp.where(eye, 1.0, 0.0)) * valid).astype(BF16).astype(F32)
    slope = logit * scores
    lean0 = jnp.sum(slope, axis=1, keepdims=True) * scale0 * scale0
    lean1_row = jnp.sum(slope, axis=0, keepdims=True) * scale1_row * scale1_row
    lean1 = jnp.sum(jnp.where(eye, lean1_row, 0.0), axis=1, keepdims=True)
    mix = logit * scale0 * warm_row
    high = mix.astype(BF16)
    low = (mix - high.astype(F32)).astype(BF16)
    high_t, low_t = high.T, low.T

    back_copies = []
    for k in range(CHUNKS):
        y0, y1 = inbox[0, :, lanes[k]], inbox[1, :, lanes[k]]
        g0 = jnp.dot(high, y1, preferred_element_type=F32)
        g0 += jnp.dot(low, y1, preferred_element_type=F32) - lean0 * y0.astype(F32)
        g1 = jnp.dot(high_t, y0, preferred_element_type=F32)
        g1 += jnp.dot(low_t, y0, preferred_element_type=F32) - lean1 * y1.astype(F32)
        for v, g in ((0, g0.astype(BF16)), (1, g1.astype(BF16))):
            grads[v, :, lanes[k]] = g
            returned[v, 0:block, lanes[k]] = g[0:block]
        copies = []
        for m in order:
            span = pl.ds(m * block, block)
            copies.append(push(
                grads.at[:, span, lanes[k]], returned.at[:, span, lanes[k]],
                b_send.at[k, m], b_recv.at[k, m], (behind[m], col),
            ))
        back_copies.append(copies)

    for x, copy in zip((2, 3, 1), f_copies):
        copy.wait_recv()
        turn_columns(x)
    across = (dp // 2) * 2 + (1 - dp % 2)
    layer, side = dp // 2, dp % 2
    layers = n_dp // 2
    x_copies, z_copies = [], []

    def finish_pair(k):
        x_copies[k].wait_recv()
        pair = terms[:, side, :, lanes[k]] + from_x[:, :, lanes[k]].astype(F32)
        pairs[:, :, lanes[k]] = pair
        pairs16[:, :, lanes[k]] = pair.astype(BF16)
        copies = []
        for step in range(layers - 1, 0, -1):
            to = lax.rem(layer + step, layers)
            copies.append(push(
                pairs16.at[to, :, lanes[k]], from_z.at[step, :, lanes[k]],
                z_send.at[k, step], z_recv.at[k, step], (to * 2 + side, col),
            ))
        z_copies.append(copies)

    for k in range(CHUNKS):
        for copy in back_copies[k]:
            copy.wait_recv()
        rows = jnp.zeros((rows2, WIDTHS[k]), F32)
        for v in range(2):
            rows += jnp.dot(pick_t[v], returned[v, :, lanes[k]], preferred_element_type=F32)
        rows = rows.astype(BF16)
        out_rows[:, lanes[k]] = rows
        gathered[0:rows2, lanes[k]] = rows
        own = gathered.at[pl.ds(0, rows2), lanes[k]]
        spans = [pl.ds(x * rows2, rows2) for x in range(4)]
        to_peer = push(
            own, gathered.at[spans[2], lanes[k]], g_send.at[1, k], g_recv.at[1, k], (dp, peer)
        )
        to_sib = push(
            own, gathered.at[spans[1], lanes[k]], g_send.at[0, k], g_recv.at[0, k], (dp, sib)
        )
        if k > 0:
            finish_pair(k - 1)
        to_peer.wait_recv()
        relay = push(
            gathered.at[spans[2], lanes[k]], gathered.at[spans[3], lanes[k]],
            g_send.at[2, k], g_recv.at[2, k], (dp, sib),
        )
        to_sib.wait_recv()
        relay.wait_recv()
        term = jnp.dot(fcols_t[...], gathered[:, lanes[k]], preferred_element_type=F32)
        term = term.reshape(layers, 2, piece, WIDTHS[k])
        terms[:, :, :, lanes[k]] = term
        terms16[:, :, :, lanes[k]] = term.astype(BF16)
        x_copies.append(push(
            terms16.at[:, 1 - side, :, lanes[k]], from_x.at[:, :, lanes[k]],
            x_send.at[k], x_recv.at[k], (across, col),
        ))
    finish_pair(CHUNKS - 1)
    for k in range(CHUNKS):
        total = pairs[layer, :, lanes[k]]
        for copy in z_copies[k]:
            copy.wait_recv()
        for step in range(1, layers):
            total += from_z[step, :, lanes[k]].astype(F32)
        out_weight[:, lanes[k]] = total / rows_dev
    for copy in sends:
        copy.wait_send()


def local_kernel(features, head_weight, bin_of_row, bin_owner, bin_link):
    rows_dev, views, feat_dim = features.shape
    part, emb = head_weight.shape
    n_dp = lax.axis_size("dp")
    bins = bin_owner.shape[0]
    per_bin = max(2, 2 * rows_dev // bins)
    block = -(-per_bin * MOSTB // 16) * 16
    slots = n_dp * block
    rows2 = rows_dev * views
    layers = n_dp // 2
    piece = part // n_dp
    vmem = pl.BlockSpec(memory_space=pltpu.VMEM)
    smem = pl.BlockSpec(memory_space=pltpu.SMEM)
    dma = pltpu.SemaphoreType.DMA
    wide = pltpu.VMEM((views, slots, emb), BF16)
    grad_rows, grad_weight = pl.pallas_call(
        functools.partial(owners_kernel, n_dp, block, per_bin, rows_dev),
        out_shape=(
            jax.ShapeDtypeStruct((rows2, emb), BF16),
            jax.ShapeDtypeStruct((piece, emb), F32),
        ),
        in_specs=[vmem, vmem, vmem, smem, smem],
        out_specs=(vmem, vmem),
        scratch_shapes=[
            pltpu.VMEM((3, part, emb), BF16),
            pltpu.VMEM((4 * rows2, part), BF16),
            pltpu.VMEM((part, 4 * rows2), BF16),
            wide, wide,
            pltpu.VMEM((slots, 128), BF16),
            pltpu.VMEM((slots, 128), BF16),
            wide, wide,
            pltpu.VMEM((4 * rows2, emb), BF16),
            pltpu.VMEM((layers, 2, piece, emb), F32),
            pltpu.VMEM((layers, 2, piece, emb), BF16),
            pltpu.VMEM((layers, piece, emb), BF16),
            pltpu.VMEM((layers, piece, emb), F32),
            pltpu.VMEM((layers, piece, emb), BF16),
            pltpu.VMEM((layers, piece, emb), BF16),
            dma((3, CHUNKS)), dma((3, CHUNKS)),
            dma((4,)), dma((4,)),
            dma((n_dp,)), dma((n_dp,)),
            dma((CHUNKS, n_dp)), dma((CHUNKS, n_dp)),
            dma((CHUNKS, n_dp)), dma((CHUNKS, n_dp)),
            dma((3, CHUNKS)), dma((3, CHUNKS)),
            dma((CHUNKS,)), dma((CHUNKS,)),
            dma((CHUNKS, layers)), dma((CHUNKS, layers)),
        ],
        compiler_params=pltpu.CompilerParams(
            collective_id=0, has_side_effects=True, vmem_limit_bytes=48 * 1024 * 1024
        ),
        cost_estimate=pl.CostEstimate(
            flops=4 * rows2 * feat_dim * emb, bytes_accessed=16 * 1024 * 1024, transcendentals=0
        ),
    )(features.reshape(rows2, feat_dim), head_weight, bin_of_row, bin_owner, bin_link)
    return grad_rows.reshape(rows_dev, views, emb), grad_weight


def solution(mesh):
    small = mesh.shape["dp"] <= 8 and mesh.shape["bin"] == 4
    return jax.shard_map(
        local_kernel if small else local,
        mesh=mesh,
        in_specs=(P(("dp", "bin"), None, None), P("bin", None), P(("dp", "bin"), None), P(), P()),
        out_specs=(P(("dp", "bin"), None, None), P(("bin", "dp"), None)),
        check_vma=False,
    )
```

```python
import functools

import jax
import jax.numpy as jnp
from jax import lax
from jax.experimental import pallas as pl
from jax.experimental.pallas import tpu as pltpu
from jax.sharding import PartitionSpec as P

MOSTB = 2


SOFTMAX_TEMP_SCALE = 0.1


def allowed_mask(valid, first, bin_link, group_slots, per_bin):
    per_owner = per_bin * MOSTB
    position = jnp.arange(group_slots, dtype=jnp.int32)
    local_bin = position % per_owner // per_bin
    padded = jnp.concatenate([bin_link, jnp.zeros((MOSTB,), jnp.int32)])
    nearby = lax.dynamic_slice(padded, (first,), (MOSTB,))
    lower = jnp.minimum(local_bin[:, None], local_bin[None, :])
    linked = jnp.zeros((group_slots, group_slots), jnp.int32)
    for height in range(MOSTB):
        linked = linked + jnp.where(lower == height, nearby[height], 0)
    spacing = jnp.abs(local_bin[:, None] - local_bin[None, :])
    paired = valid[:, None] & valid[None, :]
    allowed = paired & ((spacing == 0) | (spacing == 1) & (linked == 1))
    allowed = allowed | (position[:, None] == position[None, :])
    return allowed.astype(jnp.float32)


def contrast(query_rows, key_matrix, allowed, valid):
    similarity_scores = (
        lax.dot_general(
            query_rows, key_matrix, (((1,), (1,)), ((), ())), preferred_element_type=jnp.float32
        )
        / SOFTMAX_TEMP_SCALE
    )
    weights = allowed * jnp.exp(similarity_scores)
    shares = weights / jnp.sum(weights, axis=1, keepdims=True)
    position = jnp.arange(query_rows.shape[0], dtype=jnp.int32)
    diagonal = (position[:, None] == position[None, :]).astype(jnp.float32)
    logit_gradient = ((shares - diagonal) * valid[:, None]).astype(jnp.bfloat16)
    query_gradient = (
        jnp.dot(logit_gradient, key_matrix, preferred_element_type=jnp.float32) / SOFTMAX_TEMP_SCALE
    ).astype(jnp.bfloat16)
    key_gradient_rows = (
        lax.dot_general(
            logit_gradient, query_rows, (((0,), (0,)), ((), ())), preferred_element_type=jnp.float32
        )
        / SOFTMAX_TEMP_SCALE
    ).astype(jnp.bfloat16)
    return jnp.stack([query_gradient, key_gradient_rows], axis=1)


def local(features, head_weight, bin_of_row, bin_owner, bin_link):
    rows_dev, views, feat_dim = features.shape
    part_rows, emb_dim = head_weight.shape
    sources = lax.axis_size("dp")
    bin_count = bin_owner.shape[0]
    per_bin = max(2, 2 * rows_dev // bin_count)
    per_owner = per_bin * MOSTB
    group_slots = sources * per_owner
    flat = features.reshape(rows_dev * views, feat_dim)
    columns = flat
    folded = jnp.dot(
        columns,
        lax.all_gather(head_weight, "bin", axis=0, tiled=True),
        preferred_element_type=jnp.float32,
    )
    embedded = folded.reshape(rows_dev, views, emb_dim)
    scale = lax.rsqrt(jnp.sum(embedded * embedded, axis=2, keepdims=True) + 1e-06)
    unit = embedded * scale
    sent = unit.astype(jnp.bfloat16)
    row_bins = bin_of_row[:, 0]
    lookup = row_bins[:, None] == jnp.arange(bin_count, dtype=jnp.int32)[None, :]
    owner = jnp.sum(jnp.where(lookup, bin_owner[None, :], 0), axis=1)
    first_by_bin = jnp.sum((bin_owner[None, :] < bin_owner[:, None]).astype(jnp.int32), axis=1)
    local_bin = row_bins - jnp.sum(jnp.where(lookup, first_by_bin[None, :], 0), axis=1)
    order = jnp.arange(rows_dev, dtype=jnp.int32)
    earlier = (row_bins[:, None] == row_bins[None, :]) & (order[None, :] < order[:, None])
    seat = jnp.sum(earlier.astype(jnp.int32), axis=1)
    target = owner * per_owner + local_bin * per_bin + seat
    outbox = jnp.zeros((group_slots, views, emb_dim), jnp.bfloat16).at[target].set(sent)
    filled = (
        jnp.zeros((group_slots,), jnp.bfloat16).at[target].set(jnp.ones((rows_dev,), jnp.bfloat16))
    )
    inbox, present = (
        lax.all_to_all(
            outbox.reshape(sources, per_owner, views, emb_dim),
            "dp",
            split_axis=0,
            concat_axis=0,
            tiled=True,
        ),
        lax.all_to_all(
            filled.reshape(sources, per_owner), "dp", split_axis=0, concat_axis=0, tiled=True
        ),
    )
    inbox = inbox.reshape(group_slots, views, emb_dim)
    valid = present.reshape(group_slots) > 0.5
    first = jnp.sum((bin_owner < lax.axis_index("dp")).astype(jnp.int32))
    allowed = allowed_mask(valid, first, bin_link, group_slots, per_bin)
    grads = contrast(inbox[:, 0], inbox[:, 1], allowed, valid.astype(jnp.float32))
    returned = lax.all_to_all(
        grads.reshape(sources, per_owner, views, emb_dim),
        "dp",
        split_axis=0,
        concat_axis=0,
        tiled=True,
    )
    row_grads = returned.reshape(group_slots, views, emb_dim)[target].astype(jnp.float32)
    grad_rows = (
        scale * (row_grads - unit * jnp.sum(unit * row_grads, axis=2, keepdims=True))
    ).astype(jnp.bfloat16)
    column_start = lax.axis_index("bin") * part_rows
    trunk = lax.all_gather(features, "bin", axis=0, tiled=True)
    outgrad = lax.all_gather(grad_rows, "bin", axis=0, tiled=True)
    columns = lax.dynamic_slice_in_dim(trunk, column_start, part_rows, 2)
    count = trunk.shape[0]
    local_grad = lax.dot_general(
        columns.reshape(count * views, part_rows),
        outgrad.reshape(count * views, emb_dim),
        (((0,), (0,)), ((), ())),
        preferred_element_type=jnp.float32,
    )
    grad_weight = lax.psum_scatter(local_grad, "dp", scatter_dimension=0, tiled=True) / rows_dev
    return (grad_rows, grad_weight)


WIDTHS = (128, 256, 256, 256, 128)
CHUNKS = len(WIDTHS)
MESH = pl.DeviceIdType.MESH
F32 = jnp.float32
BF16 = jnp.bfloat16


def mixed(a, b, n):
    total, unit = 0, 1
    while unit < n:
        total = total + (a // unit + b // unit) % 2 * unit
        unit *= 2
    return total


def owners_kernel(
    n_dp, block, per_bin, rows_dev,
    feat, weight, row_bin, bin_owner, bin_link,
    out_rows, out_weight,
    wbuf, fcols, fcols_t, outbox, inbox, flag_out, flag_in, grads, returned, gathered,
    terms, terms16, from_x, pairs, pairs16, from_z,
    w_send, w_recv, f_send, f_recv, flag_send, flag_recv, a_send, a_recv,
    b_send, b_recv, g_send, g_recv, x_send, x_recv, z_send, z_recv,
):
    dp = lax.axis_index("dp")
    col = lax.axis_index("bin")
    half, core = col // 2, col % 2
    sib = half * 2 + (1 - core)
    peer = (1 - half) * 2 + core
    diag = (1 - half) * 2 + (1 - core)
    near = (col, sib, peer, diag)
    far = list(range(n_dp // 2, n_dp))
    close = list(range(1, n_dp // 2))
    first_core = [m for pair in zip(far, close) for m in pair] + far[len(close):]
    other_core = [m for pair in zip(close, far) for m in pair] + far[len(close):]
    turns = [a + core * (b - a) for a, b in zip(first_core, other_core)]
    rows2, feat_dim = feat.shape
    part = weight.shape[0]
    emb = weight.shape[1]
    slots = n_dp * block
    piece = part // n_dp
    bins = bin_owner.shape[0]
    sends = []

    def push(src, dst, send, recv, device):
        copy = pltpu.make_async_remote_copy(
            src_ref=src, dst_ref=dst, send_sem=send, recv_sem=recv,
            device_id=device, device_id_type=MESH,
        )
        copy.start()
        sends.append(copy)
        return copy

    barrier = pltpu.get_barrier_semaphore()
    for other in near[1:]:
        pl.semaphore_signal(barrier, inc=1, device_id=(dp, other), device_id_type=MESH)
    for m in range(1, n_dp):
        pl.semaphore_signal(barrier, inc=1, device_id=(mixed(dp, m, n_dp), col), device_id_type=MESH)
    pl.semaphore_wait(barrier, 3 + n_dp - 1)

    lanes = [pl.ds(sum(WIDTHS[:k]), WIDTHS[k]) for k in range(CHUNKS)]
    own_w = []
    for k in range(CHUNKS):
        to_peer = push(
            weight.at[:, lanes[k]], wbuf.at[1, :, lanes[k]],
            w_send.at[1, k], w_recv.at[1, k], (dp, peer),
        )
        to_sib = push(
            weight.at[:, lanes[k]], wbuf.at[0, :, lanes[k]],
            w_send.at[0, k], w_recv.at[0, k], (dp, sib),
        )
        own_w.append((to_sib, to_peer))

    pos = lax.broadcasted_iota(jnp.int32, (rows_dev, rows2), 0)
    lane_row = lax.broadcasted_iota(jnp.int32, (rows_dev, rows2), 1) // 2
    bin_col = jnp.broadcast_to(row_bin[...], (rows_dev, rows2))
    bin_row = jnp.sum(jnp.where(pos == lane_row, bin_col, 0), axis=0, keepdims=True)
    seat = jnp.sum(
        jnp.where((bin_col == bin_row) & (pos < lane_row), 1, 0), axis=0, keepdims=True
    )
    target = seat
    link = jnp.int32(0)
    for b in range(bins):
        owner = bin_owner[b]
        local_bin = jnp.int32(0)
        for b2 in range(b):
            local_bin = local_bin + jnp.where(bin_owner[b2] == owner, 1, 0)
        away = mixed(owner, dp, n_dp)
        target = target + jnp.where(bin_row == b, away * block + local_bin * per_bin, 0)
        if b + 1 < bins:
            link = link + jnp.where((owner == dp) & (local_bin == 0), bin_link[b], 0)
    place = lax.broadcasted_iota(jnp.int32, (slots, rows2), 0)
    view = lax.broadcasted_iota(jnp.int32, (slots, rows2), 1) % 2
    here = place == jnp.broadcast_to(target, (slots, rows2))
    pick = [
        jnp.where(here & (view == v), 1.0, 0.0).astype(F32) for v in range(2)
    ]
    flags = jnp.broadcast_to(jnp.sum(pick[0], axis=1, keepdims=True), (slots, 128)).astype(BF16)
    pick_t = [p.T.astype(BF16) for p in pick]
    pick = [p.astype(BF16) for p in pick]
    flag_out[...] = flags
    flag_in[0:block, :] = flags[0:block]
    flag_copies = []
    for m in range(1, n_dp):
        span = pl.ds(m * block, block)
        flag_copies.append(push(
            flag_out.at[span], flag_in.at[span], flag_send.at[m], flag_recv.at[m],
            (mixed(dp, m, n_dp), col),
        ))

    def exchange(src, dst, send, recv, k):
        def block_copy(m):
            span = pl.ds(pl.multiple_of(m * block, block), block)
            return pltpu.make_async_remote_copy(
                src_ref=src.at[:, span, lanes[k]], dst_ref=dst.at[:, span, lanes[k]],
                send_sem=send.at[k, m], recv_sem=recv.at[k, m],
                device_id=(mixed(dp, m, n_dp), col), device_id_type=MESH,
            )

        for m in turns:
            block_copy(m).start()
        copies = [block_copy(m) for m in range(1, n_dp)]
        sends.extend(copies)
        return copies

    def columns_of(other):
        return pl.ds(pl.multiple_of(other * part, part), part)

    out_copies = []
    for k in range(CHUNKS):
        to_sib, to_peer = own_w[k]
        to_peer.wait_recv()
        relay = push(
            wbuf.at[1, :, lanes[k]], wbuf.at[2, :, lanes[k]],
            w_send.at[2, k], w_recv.at[2, k], (dp, sib),
        )
        y = jnp.dot(feat[:, columns_of(col)], weight[:, lanes[k]], preferred_element_type=F32)
        y += jnp.dot(feat[:, columns_of(peer)], wbuf[1, :, lanes[k]], preferred_element_type=F32)
        to_sib.wait_recv()
        y += jnp.dot(feat[:, columns_of(sib)], wbuf[0, :, lanes[k]], preferred_element_type=F32)
        relay.wait_recv()
        y += jnp.dot(feat[:, columns_of(diag)], wbuf[2, :, lanes[k]], preferred_element_type=F32)
        y = y.astype(BF16)
        for v in range(2):
            placed = jnp.dot(pick[v], y, preferred_element_type=F32).astype(BF16)
            outbox[v, :, lanes[k]] = placed
            inbox[v, 0:block, lanes[k]] = placed[0:block]
        out_copies.append(exchange(outbox, inbox, a_send, a_recv, k))

    f_copies = []
    for x in (2, 3, 1):
        f_copies.append(push(
            feat.at[:, columns_of(near[x])], fcols.at[pl.ds(x * rows2, rows2), :],
            f_send.at[x], f_recv.at[x], (dp, near[x]),
        ))
    fcols[0:rows2, :] = feat[:, columns_of(col)]

    for copy in flag_copies:
        copy.wait_recv()
    s_pos = lax.broadcasted_iota(jnp.int32, (slots, slots), 0)
    t_pos = lax.broadcasted_iota(jnp.int32, (slots, slots), 1)
    eye = s_pos == t_pos
    valid = flag_in[:, 0:1].astype(F32)
    valid_row = jnp.sum(jnp.where(eye, valid, 0.0), axis=0, keepdims=True)
    s_bin = (lax.broadcasted_iota(jnp.int32, (slots, 1), 0) % block >= per_bin).astype(jnp.int32)
    t_bin = (lax.broadcasted_iota(jnp.int32, (1, slots), 1) % block >= per_bin).astype(jnp.int32)
    bound = jnp.where(s_bin == t_bin, 1.0, (link == 1).astype(F32))
    allowed = jnp.where(eye, 1.0, valid * valid_row * bound)

    def turn_columns(x):
        span = pl.ds(x * rows2, rows2)
        fcols_t[:, span] = fcols[span, :].T

    turn_columns(0)
    raw = jnp.zeros((slots, slots), F32)
    square = [jnp.zeros((slots, 1), F32) for _ in range(2)]
    for k in range(CHUNKS):
        for copy in out_copies[k]:
            copy.wait_recv()
        raw += lax.dot_general(
            inbox[0, :, lanes[k]], inbox[1, :, lanes[k]], (((1,), (1,)), ((), ())), preferred_element_type=F32
        )
        for v in range(2):
            row = inbox[v, :, lanes[k]].astype(F32)
            square[v] += jnp.sum(row * row, axis=1, keepdims=True)
    scale0 = lax.rsqrt(square[0] + 1e-06)
    scale1 = lax.rsqrt(square[1] + 1e-06)
    scale1_row = jnp.sum(jnp.where(eye, scale1, 0.0), axis=0, keepdims=True)
    warm_row = scale1_row * (1.0 / SOFTMAX_TEMP_SCALE)
    scores = raw * scale0 * warm_row
    weights = allowed * jnp.exp(scores)
    shares = weights / jnp.sum(weights, axis=1, keepdims=True)
    logit = ((shares - jnp.where(eye, 1.0, 0.0)) * valid).astype(BF16).astype(F32)
    slope = logit * scores
    lean0 = jnp.sum(slope, axis=1, keepdims=True) * scale0 * scale0
    lean1_row = jnp.sum(slope, axis=0, keepdims=True) * scale1_row * scale1_row
    lean1 = jnp.sum(jnp.where(eye, lean1_row, 0.0), axis=1, keepdims=True)
    mix = logit * scale0 * warm_row
    high = mix.astype(BF16)
    low = (mix - high.astype(F32)).astype(BF16)
    high_t, low_t = high.T, low.T

    back_copies = []
    for k in range(CHUNKS):
        y0, y1 = inbox[0, :, lanes[k]], inbox[1, :, lanes[k]]
        g0 = jnp.dot(high, y1, preferred_element_type=F32)
        g0 += jnp.dot(low, y1, preferred_element_type=F32) - lean0 * y0.astype(F32)
        g1 = jnp.dot(high_t, y0, preferred_element_type=F32)
        g1 += jnp.dot(low_t, y0, preferred_element_type=F32) - lean1 * y1.astype(F32)
        for v, g in ((0, g0.astype(BF16)), (1, g1.astype(BF16))):
            grads[v, :, lanes[k]] = g
            returned[v, 0:block, lanes[k]] = g[0:block]
        back_copies.append(exchange(grads, returned, b_send, b_recv, k))

    for x, copy in zip((2, 3, 1), f_copies):
        copy.wait_recv()
        turn_columns(x)
    across = (dp // 2) * 2 + (1 - dp % 2)
    layer, side = dp // 2, dp % 2
    layers = n_dp // 2
    x_copies, z_copies = [], []

    def finish_pair(k):
        x_copies[k].wait_recv()
        pair = terms[:, side, :, lanes[k]] + from_x[:, :, lanes[k]].astype(F32)
        pairs[:, :, lanes[k]] = pair
        pairs16[:, :, lanes[k]] = pair.astype(BF16)
        copies = []
        for step in range(layers - 1, 0, -1):
            to = lax.rem(layer + step, layers)
            copies.append(push(
                pairs16.at[to, :, lanes[k]], from_z.at[step, :, lanes[k]],
                z_send.at[k, step], z_recv.at[k, step], (to * 2 + side, col),
            ))
        z_copies.append(copies)

    for k in range(CHUNKS):
        for copy in back_copies[k]:
            copy.wait_recv()
        rows = jnp.zeros((rows2, WIDTHS[k]), F32)
        for v in range(2):
            rows += jnp.dot(pick_t[v], returned[v, :, lanes[k]], preferred_element_type=F32)
        rows = rows.astype(BF16)
        out_rows[:, lanes[k]] = rows
        gathered[0:rows2, lanes[k]] = rows
        own = gathered.at[pl.ds(0, rows2), lanes[k]]
        spans = [pl.ds(x * rows2, rows2) for x in range(4)]
        to_peer = push(
            own, gathered.at[spans[2], lanes[k]], g_send.at[1, k], g_recv.at[1, k], (dp, peer)
        )
        to_sib = push(
            own, gathered.at[spans[1], lanes[k]], g_send.at[0, k], g_recv.at[0, k], (dp, sib)
        )
        if k > 0:
            finish_pair(k - 1)
        to_peer.wait_recv()
        relay = push(
            gathered.at[spans[2], lanes[k]], gathered.at[spans[3], lanes[k]],
            g_send.at[2, k], g_recv.at[2, k], (dp, sib),
        )
        to_sib.wait_recv()
        relay.wait_recv()
        term = jnp.dot(fcols_t[...], gathered[:, lanes[k]], preferred_element_type=F32)
        term = term.reshape(layers, 2, piece, WIDTHS[k])
        terms[:, :, :, lanes[k]] = term
        terms16[:, :, :, lanes[k]] = term.astype(BF16)
        x_copies.append(push(
            terms16.at[:, 1 - side, :, lanes[k]], from_x.at[:, :, lanes[k]],
            x_send.at[k], x_recv.at[k], (across, col),
        ))
    finish_pair(CHUNKS - 1)
    for k in range(CHUNKS):
        total = pairs[layer, :, lanes[k]]
        for copy in z_copies[k]:
            copy.wait_recv()
        for step in range(1, layers):
            total += from_z[step, :, lanes[k]].astype(F32)
        out_weight[:, lanes[k]] = total / rows_dev
    for copy in sends:
        copy.wait_send()


def local_kernel(features, head_weight, bin_of_row, bin_owner, bin_link):
    rows_dev, views, feat_dim = features.shape
    part, emb = head_weight.shape
    n_dp = lax.axis_size("dp")
    bins = bin_owner.shape[0]
    per_bin = max(2, 2 * rows_dev // bins)
    block = -(-per_bin * MOSTB // 16) * 16
    slots = n_dp * block
    rows2 = rows_dev * views
    layers = n_dp // 2
    piece = part // n_dp
    vmem = pl.BlockSpec(memory_space=pltpu.VMEM)
    smem = pl.BlockSpec(memory_space=pltpu.SMEM)
    dma = pltpu.SemaphoreType.DMA
    wide = pltpu.VMEM((views, slots, emb), BF16)
    grad_rows, grad_weight = pl.pallas_call(
        functools.partial(owners_kernel, n_dp, block, per_bin, rows_dev),
        out_shape=(
            jax.ShapeDtypeStruct((rows2, emb), BF16),
            jax.ShapeDtypeStruct((piece, emb), F32),
        ),
        in_specs=[vmem, vmem, vmem, smem, smem],
        out_specs=(vmem, vmem),
        scratch_shapes=[
            pltpu.VMEM((3, part, emb), BF16),
            pltpu.VMEM((4 * rows2, part), BF16),
            pltpu.VMEM((part, 4 * rows2), BF16),
            wide, wide,
            pltpu.VMEM((slots, 128), BF16),
            pltpu.VMEM((slots, 128), BF16),
            wide, wide,
            pltpu.VMEM((4 * rows2, emb), BF16),
            pltpu.VMEM((layers, 2, piece, emb), F32),
            pltpu.VMEM((layers, 2, piece, emb), BF16),
            pltpu.VMEM((layers, piece, emb), BF16),
            pltpu.VMEM((layers, piece, emb), F32),
            pltpu.VMEM((layers, piece, emb), BF16),
            pltpu.VMEM((layers, piece, emb), BF16),
            dma((3, CHUNKS)), dma((3, CHUNKS)),
            dma((4,)), dma((4,)),
            dma((n_dp,)), dma((n_dp,)),
            dma((CHUNKS, n_dp)), dma((CHUNKS, n_dp)),
            dma((CHUNKS, n_dp)), dma((CHUNKS, n_dp)),
            dma((3, CHUNKS)), dma((3, CHUNKS)),
            dma((CHUNKS,)), dma((CHUNKS,)),
            dma((CHUNKS, layers)), dma((CHUNKS, layers)),
        ],
        compiler_params=pltpu.CompilerParams(
            collective_id=0, has_side_effects=True, vmem_limit_bytes=48 * 1024 * 1024
        ),
        cost_estimate=pl.CostEstimate(
            flops=4 * rows2 * feat_dim * emb, bytes_accessed=16 * 1024 * 1024, transcendentals=0
        ),
    )(features.reshape(rows2, feat_dim), head_weight, bin_of_row, bin_owner, bin_link)
    return grad_rows.reshape(rows_dev, views, emb), grad_weight


def solution(mesh):
    small = mesh.shape["dp"] <= 8 and mesh.shape["bin"] == 4
    return jax.shard_map(
        local_kernel if small else local,
        mesh=mesh,
        in_specs=(P(("dp", "bin"), None, None), P("bin", None), P(("dp", "bin"), None), P(), P()),
        out_specs=(P(("dp", "bin"), None, None), P(("bin", "dp"), None)),
        check_vma=False,
    )
```

```python
import functools

import jax
import jax.numpy as jnp
from jax import lax
from jax.experimental import pallas as pl
from jax.experimental.pallas import tpu as pltpu
from jax.sharding import PartitionSpec as P

MOSTB = 2


SOFTMAX_TEMP_SCALE = 0.1


def allowed_mask(valid, first, bin_link, group_slots, per_bin):
    per_owner = per_bin * MOSTB
    position = jnp.arange(group_slots, dtype=jnp.int32)
    local_bin = position % per_owner // per_bin
    padded = jnp.concatenate([bin_link, jnp.zeros((MOSTB,), jnp.int32)])
    nearby = lax.dynamic_slice(padded, (first,), (MOSTB,))
    lower = jnp.minimum(local_bin[:, None], local_bin[None, :])
    linked = jnp.zeros((group_slots, group_slots), jnp.int32)
    for height in range(MOSTB):
        linked = linked + jnp.where(lower == height, nearby[height], 0)
    spacing = jnp.abs(local_bin[:, None] - local_bin[None, :])
    paired = valid[:, None] & valid[None, :]
    allowed = paired & ((spacing == 0) | (spacing == 1) & (linked == 1))
    allowed = allowed | (position[:, None] == position[None, :])
    return allowed.astype(jnp.float32)


def contrast(query_rows, key_matrix, allowed, valid):
    similarity_scores = (
        lax.dot_general(
            query_rows, key_matrix, (((1,), (1,)), ((), ())), preferred_element_type=jnp.float32
        )
        / SOFTMAX_TEMP_SCALE
    )
    weights = allowed * jnp.exp(similarity_scores)
    shares = weights / jnp.sum(weights, axis=1, keepdims=True)
    position = jnp.arange(query_rows.shape[0], dtype=jnp.int32)
    diagonal = (position[:, None] == position[None, :]).astype(jnp.float32)
    logit_gradient = ((shares - diagonal) * valid[:, None]).astype(jnp.bfloat16)
    query_gradient = (
        jnp.dot(logit_gradient, key_matrix, preferred_element_type=jnp.float32) / SOFTMAX_TEMP_SCALE
    ).astype(jnp.bfloat16)
    key_gradient_rows = (
        lax.dot_general(
            logit_gradient, query_rows, (((0,), (0,)), ((), ())), preferred_element_type=jnp.float32
        )
        / SOFTMAX_TEMP_SCALE
    ).astype(jnp.bfloat16)
    return jnp.stack([query_gradient, key_gradient_rows], axis=1)


def local(features, head_weight, bin_of_row, bin_owner, bin_link):
    rows_dev, views, feat_dim = features.shape
    part_rows, emb_dim = head_weight.shape
    sources = lax.axis_size("dp")
    bin_count = bin_owner.shape[0]
    per_bin = max(2, 2 * rows_dev // bin_count)
    per_owner = per_bin * MOSTB
    group_slots = sources * per_owner
    flat = features.reshape(rows_dev * views, feat_dim)
    columns = flat
    folded = jnp.dot(
        columns,
        lax.all_gather(head_weight, "bin", axis=0, tiled=True),
        preferred_element_type=jnp.float32,
    )
    embedded = folded.reshape(rows_dev, views, emb_dim)
    scale = lax.rsqrt(jnp.sum(embedded * embedded, axis=2, keepdims=True) + 1e-06)
    unit = embedded * scale
    sent = unit.astype(jnp.bfloat16)
    row_bins = bin_of_row[:, 0]
    lookup = row_bins[:, None] == jnp.arange(bin_count, dtype=jnp.int32)[None, :]
    owner = jnp.sum(jnp.where(lookup, bin_owner[None, :], 0), axis=1)
    first_by_bin = jnp.sum((bin_owner[None, :] < bin_owner[:, None]).astype(jnp.int32), axis=1)
    local_bin = row_bins - jnp.sum(jnp.where(lookup, first_by_bin[None, :], 0), axis=1)
    order = jnp.arange(rows_dev, dtype=jnp.int32)
    earlier = (row_bins[:, None] == row_bins[None, :]) & (order[None, :] < order[:, None])
    seat = jnp.sum(earlier.astype(jnp.int32), axis=1)
    target = owner * per_owner + local_bin * per_bin + seat
    outbox = jnp.zeros((group_slots, views, emb_dim), jnp.bfloat16).at[target].set(sent)
    filled = (
        jnp.zeros((group_slots,), jnp.bfloat16).at[target].set(jnp.ones((rows_dev,), jnp.bfloat16))
    )
    inbox, present = (
        lax.all_to_all(
            outbox.reshape(sources, per_owner, views, emb_dim),
            "dp",
            split_axis=0,
            concat_axis=0,
            tiled=True,
        ),
        lax.all_to_all(
            filled.reshape(sources, per_owner), "dp", split_axis=0, concat_axis=0, tiled=True
        ),
    )
    inbox = inbox.reshape(group_slots, views, emb_dim)
    valid = present.reshape(group_slots) > 0.5
    first = jnp.sum((bin_owner < lax.axis_index("dp")).astype(jnp.int32))
    allowed = allowed_mask(valid, first, bin_link, group_slots, per_bin)
    grads = contrast(inbox[:, 0], inbox[:, 1], allowed, valid.astype(jnp.float32))
    returned = lax.all_to_all(
        grads.reshape(sources, per_owner, views, emb_dim),
        "dp",
        split_axis=0,
        concat_axis=0,
        tiled=True,
    )
    row_grads = returned.reshape(group_slots, views, emb_dim)[target].astype(jnp.float32)
    grad_rows = (
        scale * (row_grads - unit * jnp.sum(unit * row_grads, axis=2, keepdims=True))
    ).astype(jnp.bfloat16)
    column_start = lax.axis_index("bin") * part_rows
    trunk = lax.all_gather(features, "bin", axis=0, tiled=True)
    outgrad = lax.all_gather(grad_rows, "bin", axis=0, tiled=True)
    columns = lax.dynamic_slice_in_dim(trunk, column_start, part_rows, 2)
    count = trunk.shape[0]
    local_grad = lax.dot_general(
        columns.reshape(count * views, part_rows),
        outgrad.reshape(count * views, emb_dim),
        (((0,), (0,)), ((), ())),
        preferred_element_type=jnp.float32,
    )
    grad_weight = lax.psum_scatter(local_grad, "dp", scatter_dimension=0, tiled=True) / rows_dev
    return (grad_rows, grad_weight)


WIDTHS = (128, 256, 256, 256, 128)
CHUNKS = len(WIDTHS)
MESH = pl.DeviceIdType.MESH
F32 = jnp.float32
BF16 = jnp.bfloat16


def mixed(a, b, n):
    total, unit = 0, 1
    while unit < n:
        total = total + (a // unit + b // unit) % 2 * unit
        unit *= 2
    return total


def owners_kernel(
    n_dp, block, per_bin, rows_dev,
    feat3, weight, row_bin, bin_owner, bin_link,
    out_rows, out_weight,
    feat, wbuf, fcols, fcols_t, outbox, inbox, flag_out, flag_in, grads, returned, gathered,
    terms, terms16, from_x, pairs, pairs16, from_z,
    w_send, w_recv, f_send, f_recv, flag_send, flag_recv, a_send, a_recv,
    b_send, b_recv, g_send, g_recv, x_send, x_recv, z_send, z_recv,
):
    dp = lax.axis_index("dp")
    col = lax.axis_index("bin")
    half, core = col // 2, col % 2
    sib = half * 2 + (1 - core)
    peer = (1 - half) * 2 + core
    diag = (1 - half) * 2 + (1 - core)
    near = (col, sib, peer, diag)
    far = list(range(n_dp // 2, n_dp))
    close = list(range(1, n_dp // 2))
    first_core = [m for pair in zip(far, close) for m in pair] + far[len(close):]
    other_core = [m for pair in zip(close, far) for m in pair] + far[len(close):]
    turns = [a + core * (b - a) for a, b in zip(first_core, other_core)]
    rows2, feat_dim = feat.shape
    part = weight.shape[0]
    emb = weight.shape[1]
    slots = n_dp * block
    piece = part // n_dp
    bins = bin_owner.shape[0]
    sends = []

    def push(src, dst, send, recv, device):
        copy = pltpu.make_async_remote_copy(
            src_ref=src, dst_ref=dst, send_sem=send, recv_sem=recv,
            device_id=device, device_id_type=MESH,
        )
        copy.start()
        sends.append(copy)
        return copy

    barrier = pltpu.get_barrier_semaphore()
    for other in near[1:]:
        pl.semaphore_signal(barrier, inc=1, device_id=(dp, other), device_id_type=MESH)
    for m in range(1, n_dp):
        pl.semaphore_signal(barrier, inc=1, device_id=(mixed(dp, m, n_dp), col), device_id_type=MESH)
    pl.semaphore_wait(barrier, 3 + n_dp - 1)

    lanes = [pl.ds(sum(WIDTHS[:k]), WIDTHS[k]) for k in range(CHUNKS)]
    own_w = []
    for k in range(CHUNKS):
        to_peer = push(
            weight.at[:, lanes[k]], wbuf.at[1, :, lanes[k]],
            w_send.at[1, k], w_recv.at[1, k], (dp, peer),
        )
        to_sib = push(
            weight.at[:, lanes[k]], wbuf.at[0, :, lanes[k]],
            w_send.at[0, k], w_recv.at[0, k], (dp, sib),
        )
        own_w.append((to_sib, to_peer))

    feat[...] = feat3[...].reshape(rows2, feat_dim)

    pos = lax.broadcasted_iota(jnp.int32, (rows_dev, rows2), 0)
    lane_row = lax.broadcasted_iota(jnp.int32, (rows_dev, rows2), 1) // 2
    spot = lax.broadcasted_iota(jnp.int32, (rows_dev, rows_dev), 0)
    spot_t = lax.broadcasted_iota(jnp.int32, (rows_dev, rows_dev), 1)
    bin_col = jnp.sum(jnp.where(spot == spot_t, row_bin[...], 0), axis=1, keepdims=True)
    bin_col = jnp.broadcast_to(bin_col, (rows_dev, rows2))
    bin_row = jnp.sum(jnp.where(pos == lane_row, bin_col, 0), axis=0, keepdims=True)
    seat = jnp.sum(
        jnp.where((bin_col == bin_row) & (pos < lane_row), 1, 0), axis=0, keepdims=True
    )
    target = seat
    link = jnp.int32(0)
    for b in range(bins):
        owner = bin_owner[b]
        local_bin = jnp.int32(0)
        for b2 in range(b):
            local_bin = local_bin + jnp.where(bin_owner[b2] == owner, 1, 0)
        away = mixed(owner, dp, n_dp)
        target = target + jnp.where(bin_row == b, away * block + local_bin * per_bin, 0)
        if b + 1 < bins:
            link = link + jnp.where((owner == dp) & (local_bin == 0), bin_link[b], 0)
    place = lax.broadcasted_iota(jnp.int32, (slots, rows2), 0)
    view = lax.broadcasted_iota(jnp.int32, (slots, rows2), 1) % 2
    here = place == jnp.broadcast_to(target, (slots, rows2))
    pick = [
        jnp.where(here & (view == v), 1.0, 0.0).astype(F32) for v in range(2)
    ]
    flags = jnp.broadcast_to(jnp.sum(pick[0], axis=1, keepdims=True), (slots, 128)).astype(BF16)
    pick_t = [p.T.astype(BF16) for p in pick]
    pick = [p.astype(BF16) for p in pick]
    flag_out[...] = flags
    flag_in[0:block, :] = flags[0:block]
    flag_copies = []
    for m in range(1, n_dp):
        span = pl.ds(m * block, block)
        flag_copies.append(push(
            flag_out.at[span], flag_in.at[span], flag_send.at[m], flag_recv.at[m],
            (mixed(dp, m, n_dp), col),
        ))

    def exchange(src, dst, send, recv, k):
        def block_copy(m):
            span = pl.ds(pl.multiple_of(m * block, block), block)
            return pltpu.make_async_remote_copy(
                src_ref=src.at[:, span, lanes[k]], dst_ref=dst.at[:, span, lanes[k]],
                send_sem=send.at[k, m], recv_sem=recv.at[k, m],
                device_id=(mixed(dp, m, n_dp), col), device_id_type=MESH,
            )

        for m in turns:
            block_copy(m).start()
        copies = [block_copy(m) for m in range(1, n_dp)]
        sends.extend(copies)
        return copies

    def columns_of(other):
        return pl.ds(pl.multiple_of(other * part, part), part)

    out_copies = []
    for k in range(CHUNKS):
        to_sib, to_peer = own_w[k]
        to_peer.wait_recv()
        relay = push(
            wbuf.at[1, :, lanes[k]], wbuf.at[2, :, lanes[k]],
            w_send.at[2, k], w_recv.at[2, k], (dp, sib),
        )
        y = jnp.dot(feat[:, columns_of(col)], weight[:, lanes[k]], preferred_element_type=F32)
        y += jnp.dot(feat[:, columns_of(peer)], wbuf[1, :, lanes[k]], preferred_element_type=F32)
        to_sib.wait_recv()
        y += jnp.dot(feat[:, columns_of(sib)], wbuf[0, :, lanes[k]], preferred_element_type=F32)
        relay.wait_recv()
        y += jnp.dot(feat[:, columns_of(diag)], wbuf[2, :, lanes[k]], preferred_element_type=F32)
        y = y.astype(BF16)
        for v in range(2):
            placed = jnp.dot(pick[v], y, preferred_element_type=F32).astype(BF16)
            outbox[v, :, lanes[k]] = placed
            inbox[v, 0:block, lanes[k]] = placed[0:block]
        out_copies.append(exchange(outbox, inbox, a_send, a_recv, k))

    f_copies = []
    for x in (2, 3, 1):
        f_copies.append(push(
            feat.at[:, columns_of(near[x])], fcols.at[pl.ds(x * rows2, rows2), :],
            f_send.at[x], f_recv.at[x], (dp, near[x]),
        ))
    fcols[0:rows2, :] = feat[:, columns_of(col)]

    for copy in flag_copies:
        copy.wait_recv()
    s_pos = lax.broadcasted_iota(jnp.int32, (slots, slots), 0)
    t_pos = lax.broadcasted_iota(jnp.int32, (slots, slots), 1)
    eye = s_pos == t_pos
    valid = flag_in[:, 0:1].astype(F32)
    valid_row = jnp.sum(jnp.where(eye, valid, 0.0), axis=0, keepdims=True)
    s_bin = (lax.broadcasted_iota(jnp.int32, (slots, 1), 0) % block >= per_bin).astype(jnp.int32)
    t_bin = (lax.broadcasted_iota(jnp.int32, (1, slots), 1) % block >= per_bin).astype(jnp.int32)
    bound = jnp.where(s_bin == t_bin, 1.0, (link == 1).astype(F32))
    allowed = jnp.where(eye, 1.0, valid * valid_row * bound)

    def turn_columns(x):
        span = pl.ds(x * rows2, rows2)
        fcols_t[:, span] = fcols[span, :].T

    turn_columns(0)
    raw = jnp.zeros((slots, slots), F32)
    square = [jnp.zeros((slots, 1), F32) for _ in range(2)]
    for k in range(CHUNKS):
        for copy in out_copies[k]:
            copy.wait_recv()
        raw += lax.dot_general(
            inbox[0, :, lanes[k]], inbox[1, :, lanes[k]], (((1,), (1,)), ((), ())), preferred_element_type=F32
        )
        for v in range(2):
            row = inbox[v, :, lanes[k]].astype(F32)
            square[v] += jnp.sum(row * row, axis=1, keepdims=True)
    scale0 = lax.rsqrt(square[0] + 1e-06)
    scale1 = lax.rsqrt(square[1] + 1e-06)
    scale1_row = jnp.sum(jnp.where(eye, scale1, 0.0), axis=0, keepdims=True)
    warm_row = scale1_row * (1.0 / SOFTMAX_TEMP_SCALE)
    highs, lows, leans = [], [], []
    lean1_row = jnp.zeros((1, slots), F32)
    for m in range(n_dp):
        strip = slice(m * block, (m + 1) * block)
        score = raw[strip] * scale0[strip] * warm_row
        weights = allowed[strip] * jnp.exp(score)
        shares = weights * (1.0 / jnp.sum(weights, axis=1, keepdims=True))
        same = (
            lax.broadcasted_iota(jnp.int32, (block, slots), 0) + m * block
            == lax.broadcasted_iota(jnp.int32, (block, slots), 1)
        )
        logit = ((shares - jnp.where(same, 1.0, 0.0)) * valid[strip]).astype(BF16).astype(F32)
        slope = logit * score
        leans.append(jnp.sum(slope, axis=1, keepdims=True) * scale0[strip] * scale0[strip])
        lean1_row += jnp.sum(slope, axis=0, keepdims=True)
        mix = logit * scale0[strip] * warm_row
        highs.append(mix.astype(BF16))
        lows.append((mix - highs[-1].astype(F32)).astype(BF16))
    lean0 = jnp.concatenate(leans, axis=0)
    lean1_row = lean1_row * scale1_row * scale1_row
    lean1 = jnp.sum(jnp.where(eye, lean1_row, 0.0), axis=1, keepdims=True)
    high, low = jnp.concatenate(highs, axis=0), jnp.concatenate(lows, axis=0)
    high_t, low_t = high.T, low.T

    back_copies = []
    for k in range(CHUNKS):
        y0, y1 = inbox[0, :, lanes[k]], inbox[1, :, lanes[k]]
        g0 = jnp.dot(high, y1, preferred_element_type=F32)
        g0 += jnp.dot(low, y1, preferred_element_type=F32) - lean0 * y0.astype(F32)
        g1 = jnp.dot(high_t, y0, preferred_element_type=F32)
        g1 += jnp.dot(low_t, y0, preferred_element_type=F32) - lean1 * y1.astype(F32)
        for v, g in ((0, g0.astype(BF16)), (1, g1.astype(BF16))):
            grads[v, :, lanes[k]] = g
            returned[v, 0:block, lanes[k]] = g[0:block]
        back_copies.append(exchange(grads, returned, b_send, b_recv, k))

    for x, copy in zip((2, 3, 1), f_copies):
        copy.wait_recv()
        turn_columns(x)
    across = (dp // 2) * 2 + (1 - dp % 2)
    layer, side = dp // 2, dp % 2
    layers = n_dp // 2
    x_copies, z_copies = [], []

    def finish_pair(k):
        x_copies[k].wait_recv()
        pair = terms[:, side, :, lanes[k]] + from_x[:, :, lanes[k]].astype(F32)
        pairs[:, :, lanes[k]] = pair
        pairs16[:, :, lanes[k]] = pair.astype(BF16)
        copies = []
        for step in range(layers - 1, 0, -1):
            to = lax.rem(layer + step, layers)
            copies.append(push(
                pairs16.at[to, :, lanes[k]], from_z.at[step, :, lanes[k]],
                z_send.at[k, step], z_recv.at[k, step], (to * 2 + side, col),
            ))
        z_copies.append(copies)

    for k in range(CHUNKS):
        for copy in back_copies[k]:
            copy.wait_recv()
        rows = jnp.zeros((rows2, WIDTHS[k]), F32)
        for v in range(2):
            rows += jnp.dot(pick_t[v], returned[v, :, lanes[k]], preferred_element_type=F32)
        rows = rows.astype(BF16)
        out_rows[:, lanes[k]] = rows
        gathered[0:rows2, lanes[k]] = rows
        own = gathered.at[pl.ds(0, rows2), lanes[k]]
        spans = [pl.ds(x * rows2, rows2) for x in range(4)]
        to_peer = push(
            own, gathered.at[spans[2], lanes[k]], g_send.at[1, k], g_recv.at[1, k], (dp, peer)
        )
        to_sib = push(
            own, gathered.at[spans[1], lanes[k]], g_send.at[0, k], g_recv.at[0, k], (dp, sib)
        )
        if k > 0:
            finish_pair(k - 1)
        to_peer.wait_recv()
        relay = push(
            gathered.at[spans[2], lanes[k]], gathered.at[spans[3], lanes[k]],
            g_send.at[2, k], g_recv.at[2, k], (dp, sib),
        )
        to_sib.wait_recv()
        relay.wait_recv()
        term = jnp.dot(fcols_t[...], gathered[:, lanes[k]], preferred_element_type=F32)
        term = term.reshape(layers, 2, piece, WIDTHS[k])
        terms[:, :, :, lanes[k]] = term
        terms16[:, :, :, lanes[k]] = term.astype(BF16)
        x_copies.append(push(
            terms16.at[:, 1 - side, :, lanes[k]], from_x.at[:, :, lanes[k]],
            x_send.at[k], x_recv.at[k], (across, col),
        ))
    finish_pair(CHUNKS - 1)
    for k in range(CHUNKS):
        total = pairs[layer, :, lanes[k]]
        for copy in z_copies[k]:
            copy.wait_recv()
        for step in range(1, layers):
            total += from_z[step, :, lanes[k]].astype(F32)
        out_weight[:, lanes[k]] = total / rows_dev
    for copy in sends:
        copy.wait_send()


def local_kernel(features, head_weight, bin_of_row, bin_owner, bin_link):
    rows_dev, views, feat_dim = features.shape
    part, emb = head_weight.shape
    n_dp = lax.axis_size("dp")
    bins = bin_owner.shape[0]
    per_bin = max(2, 2 * rows_dev // bins)
    block = -(-per_bin * MOSTB // 16) * 16
    slots = n_dp * block
    rows2 = rows_dev * views
    layers = n_dp // 2
    piece = part // n_dp
    vmem = pl.BlockSpec(memory_space=pltpu.VMEM)
    smem = pl.BlockSpec(memory_space=pltpu.SMEM)
    dma = pltpu.SemaphoreType.DMA
    wide = pltpu.VMEM((views, slots, emb), BF16)
    grad_rows, grad_weight = pl.pallas_call(
        functools.partial(owners_kernel, n_dp, block, per_bin, rows_dev),
        out_shape=(
            jax.ShapeDtypeStruct((rows2, emb), BF16),
            jax.ShapeDtypeStruct((piece, emb), F32),
        ),
        in_specs=[vmem, vmem, vmem, smem, smem],
        out_specs=(vmem, vmem),
        scratch_shapes=[
            pltpu.VMEM((rows2, feat_dim), BF16),
            pltpu.VMEM((3, part, emb), BF16),
            pltpu.VMEM((4 * rows2, part), BF16),
            pltpu.VMEM((part, 4 * rows2), BF16),
            wide, wide,
            pltpu.VMEM((slots, 128), BF16),
            pltpu.VMEM((slots, 128), BF16),
            wide, wide,
            pltpu.VMEM((4 * rows2, emb), BF16),
            pltpu.VMEM((layers, 2, piece, emb), F32),
            pltpu.VMEM((layers, 2, piece, emb), BF16),
            pltpu.VMEM((layers, piece, emb), BF16),
            pltpu.VMEM((layers, piece, emb), F32),
            pltpu.VMEM((layers, piece, emb), BF16),
            pltpu.VMEM((layers, piece, emb), BF16),
            dma((3, CHUNKS)), dma((3, CHUNKS)),
            dma((4,)), dma((4,)),
            dma((n_dp,)), dma((n_dp,)),
            dma((CHUNKS, n_dp)), dma((CHUNKS, n_dp)),
            dma((CHUNKS, n_dp)), dma((CHUNKS, n_dp)),
            dma((3, CHUNKS)), dma((3, CHUNKS)),
            dma((CHUNKS,)), dma((CHUNKS,)),
            dma((CHUNKS, layers)), dma((CHUNKS, layers)),
        ],
        compiler_params=pltpu.CompilerParams(
            collective_id=0, has_side_effects=True, vmem_limit_bytes=48 * 1024 * 1024
        ),
        cost_estimate=pl.CostEstimate(
            flops=4 * rows2 * feat_dim * emb, bytes_accessed=16 * 1024 * 1024, transcendentals=0
        ),
    )(features, head_weight, bin_of_row.reshape(1, rows_dev), bin_owner, bin_link)
    return grad_rows.reshape(rows_dev, views, emb), grad_weight


def solution(mesh):
    small = mesh.shape["dp"] <= 8 and mesh.shape["bin"] == 4
    return jax.shard_map(
        local_kernel if small else local,
        mesh=mesh,
        in_specs=(P(("dp", "bin"), None, None), P("bin", None), P(("dp", "bin"), None), P(), P()),
        out_specs=(P(("dp", "bin"), None, None), P(("bin", "dp"), None)),
        check_vma=False,
    )
```

```python
import functools

import jax
import jax.numpy as jnp
from jax import lax
from jax.experimental import pallas as pl
from jax.experimental.pallas import tpu as pltpu
from jax.sharding import PartitionSpec as P

MOSTB = 2


SOFTMAX_TEMP_SCALE = 0.1


def allowed_mask(valid, first, bin_link, group_slots, per_bin):
    per_owner = per_bin * MOSTB
    position = jnp.arange(group_slots, dtype=jnp.int32)
    local_bin = position % per_owner // per_bin
    padded = jnp.concatenate([bin_link, jnp.zeros((MOSTB,), jnp.int32)])
    nearby = lax.dynamic_slice(padded, (first,), (MOSTB,))
    lower = jnp.minimum(local_bin[:, None], local_bin[None, :])
    linked = jnp.zeros((group_slots, group_slots), jnp.int32)
    for height in range(MOSTB):
        linked = linked + jnp.where(lower == height, nearby[height], 0)
    spacing = jnp.abs(local_bin[:, None] - local_bin[None, :])
    paired = valid[:, None] & valid[None, :]
    allowed = paired & ((spacing == 0) | (spacing == 1) & (linked == 1))
    allowed = allowed | (position[:, None] == position[None, :])
    return allowed.astype(jnp.float32)


def contrast(query_rows, key_matrix, allowed, valid):
    similarity_scores = (
        lax.dot_general(
            query_rows, key_matrix, (((1,), (1,)), ((), ())), preferred_element_type=jnp.float32
        )
        / SOFTMAX_TEMP_SCALE
    )
    weights = allowed * jnp.exp(similarity_scores)
    shares = weights / jnp.sum(weights, axis=1, keepdims=True)
    position = jnp.arange(query_rows.shape[0], dtype=jnp.int32)
    diagonal = (position[:, None] == position[None, :]).astype(jnp.float32)
    logit_gradient = ((shares - diagonal) * valid[:, None]).astype(jnp.bfloat16)
    query_gradient = (
        jnp.dot(logit_gradient, key_matrix, preferred_element_type=jnp.float32) / SOFTMAX_TEMP_SCALE
    ).astype(jnp.bfloat16)
    key_gradient_rows = (
        lax.dot_general(
            logit_gradient, query_rows, (((0,), (0,)), ((), ())), preferred_element_type=jnp.float32
        )
        / SOFTMAX_TEMP_SCALE
    ).astype(jnp.bfloat16)
    return jnp.stack([query_gradient, key_gradient_rows], axis=1)


def local(features, head_weight, bin_of_row, bin_owner, bin_link):
    rows_dev, views, feat_dim = features.shape
    part_rows, emb_dim = head_weight.shape
    sources = lax.axis_size("dp")
    bin_count = bin_owner.shape[0]
    per_bin = max(2, 2 * rows_dev // bin_count)
    per_owner = per_bin * MOSTB
    group_slots = sources * per_owner
    flat = features.reshape(rows_dev * views, feat_dim)
    columns = flat
    folded = jnp.dot(
        columns,
        lax.all_gather(head_weight, "bin", axis=0, tiled=True),
        preferred_element_type=jnp.float32,
    )
    embedded = folded.reshape(rows_dev, views, emb_dim)
    scale = lax.rsqrt(jnp.sum(embedded * embedded, axis=2, keepdims=True) + 1e-06)
    unit = embedded * scale
    sent = unit.astype(jnp.bfloat16)
    row_bins = bin_of_row[:, 0]
    lookup = row_bins[:, None] == jnp.arange(bin_count, dtype=jnp.int32)[None, :]
    owner = jnp.sum(jnp.where(lookup, bin_owner[None, :], 0), axis=1)
    first_by_bin = jnp.sum((bin_owner[None, :] < bin_owner[:, None]).astype(jnp.int32), axis=1)
    local_bin = row_bins - jnp.sum(jnp.where(lookup, first_by_bin[None, :], 0), axis=1)
    order = jnp.arange(rows_dev, dtype=jnp.int32)
    earlier = (row_bins[:, None] == row_bins[None, :]) & (order[None, :] < order[:, None])
    seat = jnp.sum(earlier.astype(jnp.int32), axis=1)
    target = owner * per_owner + local_bin * per_bin + seat
    outbox = jnp.zeros((group_slots, views, emb_dim), jnp.bfloat16).at[target].set(sent)
    filled = (
        jnp.zeros((group_slots,), jnp.bfloat16).at[target].set(jnp.ones((rows_dev,), jnp.bfloat16))
    )
    inbox, present = (
        lax.all_to_all(
            outbox.reshape(sources, per_owner, views, emb_dim),
            "dp",
            split_axis=0,
            concat_axis=0,
            tiled=True,
        ),
        lax.all_to_all(
            filled.reshape(sources, per_owner), "dp", split_axis=0, concat_axis=0, tiled=True
        ),
    )
    inbox = inbox.reshape(group_slots, views, emb_dim)
    valid = present.reshape(group_slots) > 0.5
    first = jnp.sum((bin_owner < lax.axis_index("dp")).astype(jnp.int32))
    allowed = allowed_mask(valid, first, bin_link, group_slots, per_bin)
    grads = contrast(inbox[:, 0], inbox[:, 1], allowed, valid.astype(jnp.float32))
    returned = lax.all_to_all(
        grads.reshape(sources, per_owner, views, emb_dim),
        "dp",
        split_axis=0,
        concat_axis=0,
        tiled=True,
    )
    row_grads = returned.reshape(group_slots, views, emb_dim)[target].astype(jnp.float32)
    grad_rows = (
        scale * (row_grads - unit * jnp.sum(unit * row_grads, axis=2, keepdims=True))
    ).astype(jnp.bfloat16)
    column_start = lax.axis_index("bin") * part_rows
    trunk = lax.all_gather(features, "bin", axis=0, tiled=True)
    outgrad = lax.all_gather(grad_rows, "bin", axis=0, tiled=True)
    columns = lax.dynamic_slice_in_dim(trunk, column_start, part_rows, 2)
    count = trunk.shape[0]
    local_grad = lax.dot_general(
        columns.reshape(count * views, part_rows),
        outgrad.reshape(count * views, emb_dim),
        (((0,), (0,)), ((), ())),
        preferred_element_type=jnp.float32,
    )
    grad_weight = lax.psum_scatter(local_grad, "dp", scatter_dimension=0, tiled=True) / rows_dev
    return (grad_rows, grad_weight)


WIDTHS = (128, 256, 256, 256, 128)
CHUNKS = len(WIDTHS)
MESH = pl.DeviceIdType.MESH
F32 = jnp.float32
BF16 = jnp.bfloat16


def mixed(a, b, n):
    total, unit = 0, 1
    while unit < n:
        total = total + (a // unit + b // unit) % 2 * unit
        unit *= 2
    return total


def owners_kernel(
    n_dp, block, per_bin, rows_dev,
    feat3, weight, row_bin, bin_owner, bin_link,
    out_rows, out_weight,
    feat, wbuf, fcols, fcols_t, outbox, inbox, flag_out, flag_in, grads, returned, gathered,
    terms, terms16, from_x, pairs, pairs16, from_z,
    w_send, w_recv, f_send, f_recv, flag_send, flag_recv, a_send, a_recv,
    b_send, b_recv, g_send, g_recv, x_send, x_recv, z_send, z_recv,
):
    dp = lax.axis_index("dp")
    col = lax.axis_index("bin")
    half, core = col // 2, col % 2
    sib = half * 2 + (1 - core)
    peer = (1 - half) * 2 + core
    diag = (1 - half) * 2 + (1 - core)
    near = (col, sib, peer, diag)
    far = list(range(n_dp // 2, n_dp))
    close = list(range(1, n_dp // 2))
    first_core = [m for pair in zip(far, close) for m in pair] + far[len(close):]
    other_core = [m for pair in zip(close, far) for m in pair] + far[len(close):]
    turns = [a + core * (b - a) for a, b in zip(first_core, other_core)]
    rows2, feat_dim = feat.shape
    part = weight.shape[0]
    emb = weight.shape[1]
    slots = n_dp * block
    piece = part // n_dp
    bins = bin_owner.shape[0]
    sends = []

    def push(src, dst, send, recv, device):
        copy = pltpu.make_async_remote_copy(
            src_ref=src, dst_ref=dst, send_sem=send, recv_sem=recv,
            device_id=device, device_id_type=MESH,
        )
        copy.start()
        sends.append(copy)
        return copy

    barrier = pltpu.get_barrier_semaphore()
    for other in near[1:]:
        pl.semaphore_signal(barrier, inc=1, device_id=(dp, other), device_id_type=MESH)
    for m in range(1, n_dp):
        pl.semaphore_signal(barrier, inc=1, device_id=(mixed(dp, m, n_dp), col), device_id_type=MESH)
    pl.semaphore_wait(barrier, 3 + n_dp - 1)

    lanes = [pl.ds(sum(WIDTHS[:k]), WIDTHS[k]) for k in range(CHUNKS)]
    own_w = []
    for k in range(CHUNKS):
        to_peer = push(
            weight.at[:, lanes[k]], wbuf[k].at[1],
            w_send.at[1, k], w_recv.at[1, k], (dp, peer),
        )
        to_sib = push(
            weight.at[:, lanes[k]], wbuf[k].at[0],
            w_send.at[0, k], w_recv.at[0, k], (dp, sib),
        )
        own_w.append((to_sib, to_peer))

    feat[...] = feat3[...].reshape(rows2, feat_dim)

    pos = lax.broadcasted_iota(jnp.int32, (rows_dev, rows2), 0)
    lane_row = lax.broadcasted_iota(jnp.int32, (rows_dev, rows2), 1) // 2
    spot = lax.broadcasted_iota(jnp.int32, (rows_dev, rows_dev), 0)
    spot_t = lax.broadcasted_iota(jnp.int32, (rows_dev, rows_dev), 1)
    bin_col = jnp.sum(jnp.where(spot == spot_t, row_bin[...], 0), axis=1, keepdims=True)
    bin_col = jnp.broadcast_to(bin_col, (rows_dev, rows2))
    bin_row = jnp.sum(jnp.where(pos == lane_row, bin_col, 0), axis=0, keepdims=True)
    seat = jnp.sum(
        jnp.where((bin_col == bin_row) & (pos < lane_row), 1, 0), axis=0, keepdims=True
    )
    target = seat
    link = jnp.int32(0)
    for b in range(bins):
        owner = bin_owner[b]
        local_bin = jnp.int32(0)
        for b2 in range(b):
            local_bin = local_bin + jnp.where(bin_owner[b2] == owner, 1, 0)
        away = mixed(owner, dp, n_dp)
        target = target + jnp.where(bin_row == b, away * block + local_bin * per_bin, 0)
        if b + 1 < bins:
            link = link + jnp.where((owner == dp) & (local_bin == 0), bin_link[b], 0)
    place = lax.broadcasted_iota(jnp.int32, (slots, rows2), 0)
    view = lax.broadcasted_iota(jnp.int32, (slots, rows2), 1) % 2
    here = place == jnp.broadcast_to(target, (slots, rows2))
    pick = [
        jnp.where(here & (view == v), 1.0, 0.0).astype(F32) for v in range(2)
    ]
    flags = jnp.broadcast_to(jnp.sum(pick[0], axis=1, keepdims=True), (slots, 128)).astype(BF16)
    pick_t = [p.T.astype(BF16) for p in pick]
    pick = [p.astype(BF16) for p in pick]
    flag_out[...] = flags
    flag_in[0:block, :] = flags[0:block]
    flag_copies = []
    for m in range(1, n_dp):
        span = pl.ds(m * block, block)
        flag_copies.append(push(
            flag_out.at[span], flag_in.at[span], flag_send.at[m], flag_recv.at[m],
            (mixed(dp, m, n_dp), col),
        ))

    def exchange(src, dst, send, recv, k):
        def block_copy(m):
            span = pl.ds(pl.multiple_of(m * block, block), block)
            return pltpu.make_async_remote_copy(
                src_ref=src[k].at[:, span, :], dst_ref=dst[k].at[:, span, :],
                send_sem=send.at[k, m], recv_sem=recv.at[k, m],
                device_id=(mixed(dp, m, n_dp), col), device_id_type=MESH,
            )

        for m in turns:
            block_copy(m).start()
        copies = [block_copy(m) for m in range(1, n_dp)]
        sends.extend(copies)
        return copies

    def columns_of(other):
        return pl.ds(pl.multiple_of(other * part, part), part)

    out_copies = []
    for k in range(CHUNKS):
        to_sib, to_peer = own_w[k]
        to_peer.wait_recv()
        relay = push(
            wbuf[k].at[1], wbuf[k].at[2],
            w_send.at[2, k], w_recv.at[2, k], (dp, sib),
        )
        y = jnp.dot(feat[:, columns_of(col)], weight[:, lanes[k]], preferred_element_type=F32)
        y += jnp.dot(feat[:, columns_of(peer)], wbuf[k][1], preferred_element_type=F32)
        to_sib.wait_recv()
        y += jnp.dot(feat[:, columns_of(sib)], wbuf[k][0], preferred_element_type=F32)
        relay.wait_recv()
        y += jnp.dot(feat[:, columns_of(diag)], wbuf[k][2], preferred_element_type=F32)
        y = y.astype(BF16)
        for v in range(2):
            placed = jnp.dot(pick[v], y, preferred_element_type=F32).astype(BF16)
            outbox[k][v] = placed
            inbox[k][v, 0:block, :] = placed[0:block]
        out_copies.append(exchange(outbox, inbox, a_send, a_recv, k))

    f_copies = []
    for x in (2, 3, 1):
        f_copies.append(push(
            feat.at[:, columns_of(near[x])], fcols.at[pl.ds(x * rows2, rows2), :],
            f_send.at[x], f_recv.at[x], (dp, near[x]),
        ))
    fcols[0:rows2, :] = feat[:, columns_of(col)]

    for copy in flag_copies:
        copy.wait_recv()
    s_pos = lax.broadcasted_iota(jnp.int32, (slots, slots), 0)
    t_pos = lax.broadcasted_iota(jnp.int32, (slots, slots), 1)
    eye = s_pos == t_pos
    valid = flag_in[:, 0:1].astype(F32)
    valid_row = jnp.sum(jnp.where(eye, valid, 0.0), axis=0, keepdims=True)
    s_bin = (lax.broadcasted_iota(jnp.int32, (slots, 1), 0) % block >= per_bin).astype(jnp.int32)
    t_bin = (lax.broadcasted_iota(jnp.int32, (1, slots), 1) % block >= per_bin).astype(jnp.int32)
    bound = jnp.where(s_bin == t_bin, 1.0, (link == 1).astype(F32))
    allowed = jnp.where(eye, 1.0, valid * valid_row * bound)

    def turn_columns(x):
        span = pl.ds(x * rows2, rows2)
        fcols_t[:, span] = fcols[span, :].T

    turn_columns(0)
    raw = jnp.zeros((slots, slots), F32)
    square = [jnp.zeros((slots, 1), F32) for _ in range(2)]
    for k in range(CHUNKS):
        for copy in out_copies[k]:
            copy.wait_recv()
        raw += lax.dot_general(
            inbox[k][0], inbox[k][1], (((1,), (1,)), ((), ())), preferred_element_type=F32
        )
        for v in range(2):
            row = inbox[k][v].astype(F32)
            square[v] += jnp.sum(row * row, axis=1, keepdims=True)
    scale0 = lax.rsqrt(square[0] + 1e-06)
    scale1 = lax.rsqrt(square[1] + 1e-06)
    scale1_row = jnp.sum(jnp.where(eye, scale1, 0.0), axis=0, keepdims=True)
    warm_row = scale1_row * (1.0 / SOFTMAX_TEMP_SCALE)
    highs, lows, leans = [], [], []
    lean1_row = jnp.zeros((1, slots), F32)
    for m in range(n_dp):
        strip = slice(m * block, (m + 1) * block)
        score = raw[strip] * scale0[strip] * warm_row
        weights = allowed[strip] * jnp.exp(score)
        shares = weights * (1.0 / jnp.sum(weights, axis=1, keepdims=True))
        same = (
            lax.broadcasted_iota(jnp.int32, (block, slots), 0) + m * block
            == lax.broadcasted_iota(jnp.int32, (block, slots), 1)
        )
        logit = ((shares - jnp.where(same, 1.0, 0.0)) * valid[strip]).astype(BF16).astype(F32)
        slope = logit * score
        leans.append(jnp.sum(slope, axis=1, keepdims=True) * scale0[strip] * scale0[strip])
        lean1_row += jnp.sum(slope, axis=0, keepdims=True)
        mix = logit * scale0[strip] * warm_row
        highs.append(mix.astype(BF16))
        lows.append((mix - highs[-1].astype(F32)).astype(BF16))
    lean0 = jnp.concatenate(leans, axis=0)
    lean1_row = lean1_row * scale1_row * scale1_row
    lean1 = jnp.sum(jnp.where(eye, lean1_row, 0.0), axis=1, keepdims=True)
    high, low = jnp.concatenate(highs, axis=0), jnp.concatenate(lows, axis=0)
    high_t, low_t = high.T, low.T

    back_copies = []
    for k in range(CHUNKS):
        y0, y1 = inbox[k][0], inbox[k][1]
        g0 = jnp.dot(high, y1, preferred_element_type=F32)
        g0 += jnp.dot(low, y1, preferred_element_type=F32) - lean0 * y0.astype(F32)
        g1 = jnp.dot(high_t, y0, preferred_element_type=F32)
        g1 += jnp.dot(low_t, y0, preferred_element_type=F32) - lean1 * y1.astype(F32)
        for v, g in ((0, g0.astype(BF16)), (1, g1.astype(BF16))):
            grads[k][v] = g
            returned[k][v, 0:block, :] = g[0:block]
        back_copies.append(exchange(grads, returned, b_send, b_recv, k))

    for x, copy in zip((2, 3, 1), f_copies):
        copy.wait_recv()
        turn_columns(x)
    across = (dp // 2) * 2 + (1 - dp % 2)
    layer, side = dp // 2, dp % 2
    layers = n_dp // 2
    x_copies, z_copies = [], []

    def finish_pair(k):
        x_copies[k].wait_recv()
        pair = terms[:, side, :, lanes[k]] + from_x[k][...].astype(F32)
        pairs[:, :, lanes[k]] = pair
        pairs16[k][...] = pair.astype(BF16)
        copies = []
        for step in range(layers - 1, 0, -1):
            to = lax.rem(layer + step, layers)
            copies.append(push(
                pairs16[k].at[to], from_z[k].at[step],
                z_send.at[k, step], z_recv.at[k, step], (to * 2 + side, col),
            ))
        z_copies.append(copies)

    for k in range(CHUNKS):
        for copy in back_copies[k]:
            copy.wait_recv()
        rows = jnp.zeros((rows2, WIDTHS[k]), F32)
        for v in range(2):
            rows += jnp.dot(pick_t[v], returned[k][v], preferred_element_type=F32)
        rows = rows.astype(BF16)
        out_rows[:, lanes[k]] = rows
        gathered[k][0:rows2, :] = rows
        own = gathered[k].at[pl.ds(0, rows2), :]
        spans = [pl.ds(x * rows2, rows2) for x in range(4)]
        to_peer = push(
            own, gathered[k].at[spans[2], :], g_send.at[1, k], g_recv.at[1, k], (dp, peer)
        )
        to_sib = push(
            own, gathered[k].at[spans[1], :], g_send.at[0, k], g_recv.at[0, k], (dp, sib)
        )
        if k > 0:
            finish_pair(k - 1)
        to_peer.wait_recv()
        relay = push(
            gathered[k].at[spans[2], :], gathered[k].at[spans[3], :],
            g_send.at[2, k], g_recv.at[2, k], (dp, sib),
        )
        to_sib.wait_recv()
        relay.wait_recv()
        term = jnp.dot(fcols_t[...], gathered[k][...], preferred_element_type=F32)
        term = term.reshape(layers, 2, piece, WIDTHS[k])
        terms[:, :, :, lanes[k]] = term
        terms16[k][...] = term.astype(BF16)
        x_copies.append(push(
            terms16[k].at[:, 1 - side], from_x[k],
            x_send.at[k], x_recv.at[k], (across, col),
        ))
    finish_pair(CHUNKS - 1)
    for k in range(CHUNKS):
        total = pairs[layer, :, lanes[k]]
        for copy in z_copies[k]:
            copy.wait_recv()
        for step in range(1, layers):
            total += from_z[k][step].astype(F32)
        out_weight[:, lanes[k]] = total / rows_dev
    for copy in sends:
        copy.wait_send()


def local_kernel(features, head_weight, bin_of_row, bin_owner, bin_link):
    rows_dev, views, feat_dim = features.shape
    part, emb = head_weight.shape
    n_dp = lax.axis_size("dp")
    bins = bin_owner.shape[0]
    per_bin = max(2, 2 * rows_dev // bins)
    block = -(-per_bin * MOSTB // 16) * 16
    slots = n_dp * block
    rows2 = rows_dev * views
    layers = n_dp // 2
    piece = part // n_dp
    vmem = pl.BlockSpec(memory_space=pltpu.VMEM)
    smem = pl.BlockSpec(memory_space=pltpu.SMEM)
    dma = pltpu.SemaphoreType.DMA

    def chunked(*shape):
        return tuple(pltpu.VMEM((*shape, width), BF16) for width in WIDTHS)

    wide = chunked(views, slots)
    grad_rows, grad_weight = pl.pallas_call(
        functools.partial(owners_kernel, n_dp, block, per_bin, rows_dev),
        out_shape=(
            jax.ShapeDtypeStruct((rows2, emb), BF16),
            jax.ShapeDtypeStruct((piece, emb), F32),
        ),
        in_specs=[vmem, vmem, vmem, smem, smem],
        out_specs=(vmem, vmem),
        scratch_shapes=[
            pltpu.VMEM((rows2, feat_dim), BF16),
            chunked(3, part),
            pltpu.VMEM((4 * rows2, part), BF16),
            pltpu.VMEM((part, 4 * rows2), BF16),
            wide, wide,
            pltpu.VMEM((slots, 128), BF16),
            pltpu.VMEM((slots, 128), BF16),
            wide, wide,
            chunked(4 * rows2),
            pltpu.VMEM((layers, 2, piece, emb), F32),
            chunked(layers, 2, piece),
            chunked(layers, piece),
            pltpu.VMEM((layers, piece, emb), F32),
            chunked(layers, piece),
            chunked(layers, piece),
            dma((3, CHUNKS)), dma((3, CHUNKS)),
            dma((4,)), dma((4,)),
            dma((n_dp,)), dma((n_dp,)),
            dma((CHUNKS, n_dp)), dma((CHUNKS, n_dp)),
            dma((CHUNKS, n_dp)), dma((CHUNKS, n_dp)),
            dma((3, CHUNKS)), dma((3, CHUNKS)),
            dma((CHUNKS,)), dma((CHUNKS,)),
            dma((CHUNKS, layers)), dma((CHUNKS, layers)),
        ],
        compiler_params=pltpu.CompilerParams(
            collective_id=0, has_side_effects=True, vmem_limit_bytes=48 * 1024 * 1024
        ),
        cost_estimate=pl.CostEstimate(
            flops=4 * rows2 * feat_dim * emb, bytes_accessed=16 * 1024 * 1024, transcendentals=0
        ),
    )(features, head_weight, bin_of_row.reshape(1, rows_dev), bin_owner, bin_link)
    return grad_rows.reshape(rows_dev, views, emb), grad_weight


def solution(mesh):
    small = mesh.shape["dp"] <= 8 and mesh.shape["bin"] == 4
    return jax.shard_map(
        local_kernel if small else local,
        mesh=mesh,
        in_specs=(P(("dp", "bin"), None, None), P("bin", None), P(("dp", "bin"), None), P(), P()),
        out_specs=(P(("dp", "bin"), None, None), P(("bin", "dp"), None)),
        check_vma=False,
    )
```
